256 devices in a mesh: layer: 4 (over y), grid: 64 (over x, z, core).
Axes of the slice: x: 4, y: 4, z: 8, core: 2. Of those that a mesh axis runs over, the one named last changes fastest.
Arguments:
- density: bfloat16 [512, 128, 1024], P('grid'), may hold values from -0.75 to 0.75
- pattern: int32 [512, 8], replicated, may hold values from 0 to 511, as said below
Outputs:
- purified: float32 [512, 128, 1024], P('grid', None, 'layer')
The draws below stay inside these ranges and needn't reach their ends.
Inputs may be any that keep to these rules, and one draw needn't show every extreme that they name: `pattern`: row i lists 8 different block columns, i itself among them, each of the form (i + o) mod 512 with -8 <= o <= 8.
All inputs are finite; a program needn't handle non-finite values.
Results may differ from the reference program's by a relative error of at most 0.0029.
Values may be sent and summed in bfloat16 or wider, within the bound.
No kernel may reach another device: no remote copies, remote signals or barrier semaphores. Data moves between devices by JAX's collectives and lax.ppermute only.
A program may use at most 64 MiB of HBM per device.

```python
import jax
import jax.numpy as jnp
from jax import lax

BS = 128
K = 8
BAND = 8
NB = 512


def draw_pattern(key, part):
    key = jax.random.fold_in(key, 7)
    offset_count = 2 * BAND
    scores = jax.random.randint(key, (NB, offset_count), 0, 1 << 16) * offset_count + jnp.arange(offset_count, dtype=jnp.int32)[None, :]
    picked = lax.top_k(scores, K - 1)[1].astype(jnp.int32)
    offsets = jnp.where(picked < BAND, picked - BAND, picked - BAND + 1)
    offsets = jnp.concatenate([jnp.zeros((NB, 1), jnp.int32), offsets], 1)
    row_ids = jnp.arange(NB, dtype=jnp.int32)[:, None]
    return ((row_ids + offsets) % NB).astype(jnp.int32)


def block_scale(rng, extent, split, smallest, top_value):
    gain = 1.0
    for dim, blocks in split:
        heights = jax.random.uniform(jax.random.fold_in(jax.random.fold_in(rng, 6), dim), (blocks,), jnp.float32, smallest / len(split), top_value / len(split))
        gain = gain * jnp.repeat(jnp.exp(heights), extent[dim] // blocks).reshape((-1,) + (1,) * (len(extent) - 1 - dim))
    return gain


def scatter_about(rng, shape, deviation, most, cuts=(), held_as=jnp.bfloat16):
    values = deviation * jax.random.normal(rng, shape, jnp.float32)
    if cuts:
        values = values * block_scale(rng, shape, cuts, -0.22, 0.18)
    return jnp.clip(values, -most, most).astype(held_as)


def setup_inputs(seed: int = 0) -> dict:
    key_list = jax.random.split(jax.random.key(seed), 3)
    density = scatter_about(key_list[0], (NB, BS, K * BS), (K * BS // 14) ** -0.5, 0.75, ((0, 64),))
    pattern = draw_pattern(jax.random.fold_in(key_list[2], 71), 0)
    return {"density": density, "pattern": pattern}


def multiply(left_side, right_side, pattern, selector):
    blocks = pattern.shape[0]

    def one_row(row_index):
        fetched = jnp.take(right_side, pattern[row_index], axis=0)
        aligned = jnp.einsum("abj,aybz->ayjz", selector[row_index], fetched, precision=lax.Precision.HIGHEST)
        return jnp.einsum("xay,ayjz->xjz", left_side[row_index], aligned, precision=lax.Precision.HIGHEST)

    return lax.map(one_row, jnp.arange(blocks, dtype=jnp.int32))


def reference(density, pattern):
    blocks, block_size, span_cols = density.shape
    listed = pattern.shape[1]
    values = density.astype(jnp.float32).reshape(blocks, block_size, listed, block_size)
    neighbours = jnp.take(pattern, pattern, axis=0)
    selector = (neighbours[:, :, :, None] == pattern[:, None, None, :]).astype(jnp.float32)
    square = lax.optimization_barrier(multiply(values, values, pattern, selector).astype(jnp.bfloat16))
    cube_part = multiply(square.astype(jnp.float32), values, pattern, selector)
    result = 3.0 * square.astype(jnp.float32) - 2.0 * cube_part
    return result.reshape(blocks, block_size, span_cols)
```

```python
import jax
import jax.numpy as jnp
from jax import lax
from jax.experimental import pallas as pl
from jax.experimental.pallas import tpu as pltpu
from jax.sharding import PartitionSpec as P

ROWS = 8
LISTED = 8
BS = 128
ZERO = 3 * ROWS * LISTED


def locate(pattern, grid_index):
    blocks = pattern.shape[0]
    first = grid_index * ROWS
    ring = jnp.concatenate([pattern[-ROWS:], pattern, pattern[:ROWS]], axis=0)
    window = lax.dynamic_slice_in_dim(ring, first, 3 * ROWS, 0)
    rel = (window - first + ROWS) % blocks
    rel = jnp.where(rel >= blocks // 2, rel - blocks, rel)
    own = rel[ROWS : 2 * ROWS]
    chosen = own[:, :, None] == jnp.arange(3 * ROWS, dtype=jnp.int32)
    listed = jnp.sum(jnp.where(chosen[..., None], rel[None, None], 0), axis=2)
    same = listed[:, :, None, :] == own[:, None, :, None]
    slot = jnp.sum(jnp.where(same, jnp.arange(LISTED, dtype=jnp.int32), 0), axis=3)
    place = own[:, :, None] * LISTED + slot
    return jnp.where(jnp.any(same, axis=3), place, ZERO).reshape(-1)


def kernel(meta, loc, own, inner, near, swapped, far, out, buf, square, result, sems, out_sems):
    parity, layer = meta[0], meta[1]
    half = lax.rem(layer, 2)
    outer_base = 16 * parity
    inner_base = 16 - outer_base
    sender = 1 - parity

    copies = [
        pltpu.make_async_copy(own, buf.at[pl.ds(ROWS, ROWS)], sems.at[0]),
        pltpu.make_async_copy(inner, buf.at[pl.ds(inner_base, ROWS)], sems.at[1]),
        pltpu.make_async_copy(near, buf.at[pl.ds(outer_base + 4 * sender + 2 * half, 2)], sems.at[2]),
        pltpu.make_async_copy(
            swapped, buf.at[pl.ds(outer_base + 4 * sender + 2 * (1 - half), 2)], sems.at[3]
        ),
        pltpu.make_async_copy(far, buf.at[pl.ds(outer_base + 4 * parity, 4)], sems.at[4]),
    ]
    for copy in copies:
        copy.start()
    buf[3 * ROWS, :, :BS] = jnp.zeros((BS, BS), jnp.bfloat16)
    for copy in copies:
        copy.wait()

    def block(i, c, a):
        place = loc[i * (LISTED * LISTED) + c * LISTED + a]
        start = pl.multiple_of(lax.rem(place, LISTED) * BS, BS)
        return buf[lax.div(place, LISTED), :, pl.ds(start, BS)]

    def tile(i, c, a):
        return jnp.concatenate(
            [
                jnp.concatenate([block(i, c, a), block(i, c, a + 1)], axis=1),
                jnp.concatenate([block(i, c + 1, a), block(i, c + 1, a + 1)], axis=1),
            ],
            axis=0,
        )

    def times(left, i, a):
        total = jnp.zeros((BS, 2 * BS), jnp.float32)
        for c in range(0, LISTED, 2):
            total += jnp.dot(
                left(c), tile(i, c, a), preferred_element_type=jnp.float32
            )
        return total

    def one_row(i, carry):
        for a in range(0, LISTED, 2):
            part = times(lambda c: buf[ROWS + i, :, c * BS : (c + 2) * BS], i, a)
            square[:, a * BS : (a + 2) * BS] = part.astype(jnp.bfloat16)
        cube = times(lambda c: square[:, c * BS : (c + 2) * BS], i, 2 * layer)
        start = pl.multiple_of(layer * 2 * BS, 2 * BS)
        result[i] = 3.0 * square[:, pl.ds(start, 2 * BS)].astype(jnp.float32) - 2.0 * cube
        pltpu.make_async_copy(result.at[i], out.at[i], out_sems.at[i]).start()
        return carry

    lax.fori_loop(0, ROWS, one_row, 0)
    for i in range(ROWS):
        pltpu.make_async_copy(result.at[i], out.at[i], out_sems.at[i]).wait()


def local(density, pattern):
    grid = lax.axis_size("grid")
    layers = lax.axis_size("layer")
    g = lax.axis_index("grid")
    layer = lax.axis_index("layer")
    parity = g % 2
    half = layer % 2
    outer_pairs = [(i, (i - 1) % grid if i % 2 == 0 else (i + 1) % grid) for i in range(grid)]
    inner_pairs = [(i, i + 1 if i % 2 == 0 else i - 1) for i in range(grid)]
    swap_pairs = []
    for y in range(layers):
        for i in range(grid):
            other = (y ^ 1) if i % 2 == 0 else ((y + 1) ^ 1) - 1
            swap_pairs.append((y * grid + i, (other % layers) * grid + i))
    near_send = lax.dynamic_slice_in_dim(density, 4 * parity + 2 * half, 2, 0)
    near = lax.ppermute(near_send, "grid", outer_pairs)
    far_send = lax.dynamic_slice_in_dim(density, 4 * (1 - parity), 4, 0)
    far = lax.ppermute(far_send, "grid", outer_pairs)
    inner = lax.ppermute(density, "grid", inner_pairs)
    swapped = lax.ppermute(near, ("layer", "grid"), swap_pairs)
    loc = locate(pattern, g)
    meta = jnp.stack([parity, layer]).astype(jnp.int32)
    any_space = pl.BlockSpec(memory_space=pl.ANY)
    smem = pl.BlockSpec(memory_space=pltpu.SMEM)
    return pl.pallas_call(
        kernel,
        out_shape=jax.ShapeDtypeStruct((ROWS, BS, 2 * BS), jnp.float32),
        in_specs=[smem, smem] + [any_space] * 5,
        out_specs=any_space,
        scratch_shapes=[
            pltpu.VMEM((3 * ROWS + 1, BS, LISTED * BS), jnp.bfloat16),
            pltpu.VMEM((BS, LISTED * BS), jnp.bfloat16),
            pltpu.VMEM((ROWS, BS, 2 * BS), jnp.float32),
            pltpu.SemaphoreType.DMA((5,)),
            pltpu.SemaphoreType.DMA((ROWS,)),
        ],
        compiler_params=pltpu.CompilerParams(vmem_limit_bytes=16 * 1024 * 1024),
        cost_estimate=pl.CostEstimate(flops=2_700_000_000, bytes_accessed=8_000_000, transcendentals=0),
    )(meta, loc, density, inner, near, swapped, far)


def solution(mesh):
    placed = (P("grid", None, None), P())
    return jax.shard_map(
        local, mesh=mesh, in_specs=placed, out_specs=P("grid", None, "layer"), check_vma=False
    )
```

```python
import jax
import jax.numpy as jnp
from jax import lax
from jax.experimental import pallas as pl
from jax.experimental.pallas import tpu as pltpu
from jax.sharding import PartitionSpec as P

ROWS = 8
HALF = ROWS // 2
LISTED = 8
BS = 128
SPAN = LISTED * BS
WINDOW = 3 * ROWS
STRIDE = WINDOW + 1
ZERO = WINDOW
COLUMNS = 5 * ROWS
ANY = pl.BlockSpec(memory_space=pl.ANY)
HBM = pl.BlockSpec(memory_space=pltpu.HBM)
SMEM = pl.BlockSpec(memory_space=pltpu.SMEM)
VMEM = pl.BlockSpec(memory_space=pltpu.VMEM)


def tables(pattern, grid_index):
    blocks = pattern.shape[0]
    first = grid_index * ROWS
    ring = jnp.concatenate([pattern[-ROWS:], pattern, pattern[:ROWS]], axis=0)
    window = lax.dynamic_slice_in_dim(ring, first, WINDOW, 0)
    rel = window - first + 2 * ROWS
    rel = jnp.where(rel >= blocks // 2, rel - blocks, rel)
    rel = jnp.where(rel < -blocks // 2, rel + blocks, rel)
    listed = rel[ROWS : 2 * ROWS] - ROWS
    rows = lax.broadcasted_iota(jnp.int32, (STRIDE, COLUMNS), 0)
    cols = lax.broadcasted_iota(jnp.int32, (STRIDE, COLUMNS), 1)
    padded = jnp.concatenate([rel, jnp.full((1, LISTED), -1, jnp.int32)], axis=0)
    place = jnp.full((STRIDE, COLUMNS), ZERO, jnp.int32)
    for b in range(LISTED):
        place = jnp.where(padded[:, b : b + 1] == cols, b * STRIDE + rows, place)
    return listed.reshape(-1), place.reshape(-1)


def pick_kernel(count, near, source, out, sem):
    parity = lax.rem(lax.axis_index("grid"), 2)
    if near:
        start = HALF * parity + count * lax.rem(lax.axis_index("layer"), 2)
    else:
        start = HALF * (1 - parity)
    copy = pltpu.make_async_copy(source.at[pl.ds(start, count)], out, sem)
    copy.start()
    copy.wait()


def pick(density, count, near):
    return pl.pallas_call(
        lambda *refs: pick_kernel(count, near, *refs),
        out_shape=jax.ShapeDtypeStruct((count, BS, SPAN), density.dtype),
        in_specs=[HBM],
        out_specs=ANY,
        scratch_shapes=[pltpu.SemaphoreType.DMA],
        compiler_params=pltpu.CompilerParams(vmem_limit_bytes=2**20),
        name="pick_near" if near else "pick_far",
    )(density)


def place_rows(source, count, store, first, sem):
    return [
        pltpu.make_async_copy(
            source.at[:, :, pl.ds(s * BS, BS)], store.at[pl.ds(s * STRIDE + first, count)], sem.at[s]
        )
        for s in range(LISTED)
    ]


class Blocks:
    def __init__(self, listed, place, store, i):
        self.listed, self.place, self.store, self.i = listed, place, store, i

    def row(self, c):
        return self.listed[self.i * LISTED + c]

    def block(self, row, a):
        return self.store[self.place[row * COLUMNS + self.row(a) + ROWS]]

    def pair(self, row, a):
        return jnp.concatenate([self.block(row, a), self.block(row, a + 1)], axis=1)

    def times(self, left, rows, a):
        total = jnp.zeros((BS, 2 * BS), jnp.float32)
        for c in range(0, LISTED, 2):
            right = jnp.concatenate([self.pair(rows[c], a), self.pair(rows[c + 1], a)], axis=0)
            total += jnp.dot(left(c), right, preferred_element_type=jnp.float32)
        return total


def add_rows(blocks, own, i, low, total):
    for c in range(LISTED):
        row = blocks.row(c)

        @pl.when(jnp.logical_and(row >= low, row < low + HALF))
        def _():
            left = own[i, :, c * BS : (c + 1) * BS]
            for a in range(0, LISTED, 2):
                total[:, a * BS : (a + 2) * BS] += jnp.dot(
                    left, blocks.pair(row, a), preferred_element_type=jnp.float32
                )


def finish(blocks, total, square, result):
    layer = lax.axis_index("layer")
    square[...] = total[...].astype(jnp.bfloat16)
    rows = [blocks.row(c) for c in range(LISTED)]
    cube = blocks.times(lambda c: square[:, c * BS : (c + 2) * BS], rows, 2 * layer)
    start = pl.multiple_of(layer * 2 * BS, 2 * BS)
    result[...] = 3.0 * square[:, pl.ds(start, 2 * BS)].astype(jnp.float32) - 2.0 * cube


def close_kernel(listed, place, own, inner, store, partial, sems):
    parity = lax.rem(lax.axis_index("grid"), 2)
    outer = 2 * ROWS * parity
    copies = place_rows(own, ROWS, store, ROWS, sems.at[0])
    copies += place_rows(inner, ROWS, store, 2 * ROWS - outer, sems.at[1])
    for copy in copies:
        copy.start()
    store[ZERO] = jnp.zeros((BS, BS), jnp.bfloat16)
    for copy in copies:
        copy.wait()

    def one_row(i, carry):
        blocks = Blocks(listed, place, store, i)
        rows = []
        for c in range(LISTED):
            row = blocks.row(c)
            away = jnp.logical_and(row >= outer, row < outer + ROWS)
            rows.append(jnp.where(away, WINDOW, row))
        for a in range(0, LISTED, 2):
            partial[i, :, a * BS : (a + 2) * BS] = blocks.times(
                lambda c: own[i, :, c * BS : (c + 2) * BS], rows, a
            )
        return carry

    lax.fori_loop(0, ROWS, one_row, 0)


def near_kernel(listed, place, own, near, swapped, partial, _, store, rest, out, total, square, result, sems, out_sems):
    parity = lax.rem(lax.axis_index("grid"), 2)
    half = lax.rem(lax.axis_index("layer"), 2)
    low = 2 * ROWS * parity + HALF * (1 - parity)
    copies = place_rows(near, 2, store, low + 2 * half, sems.at[0])
    copies += place_rows(swapped, 2, store, low + 2 * (1 - half), sems.at[1])
    for copy in copies:
        copy.start()
    for copy in copies:
        copy.wait()

    def unfinished(e, carry):
        i = jnp.where(parity == 0, e, ROWS - 1 - e)
        rest[e] = partial[i]
        add_rows(Blocks(listed, place, store, i), own, i, low, rest.at[e])
        return carry

    def finished(e, carry):
        i = jnp.where(parity == 0, e, ROWS - 1 - e)
        blocks = Blocks(listed, place, store, i)
        total[...] = partial[i]
        add_rows(blocks, own, i, low, total)
        finish(blocks, total, square, result.at[e - HALF])
        pltpu.make_async_copy(result.at[e - HALF], out.at[i], out_sems.at[e - HALF]).start()
        return carry

    lax.fori_loop(HALF, ROWS, finished, 0)
    lax.fori_loop(0, HALF, unfinished, 0)
    for e in range(HALF):
        pltpu.make_async_copy(result.at[e], out.at[0], out_sems.at[e]).wait()


def far_kernel(listed, place, own, far, rest, _s, _o, store, out, total, square, result, sems, out_sems):
    parity = lax.rem(lax.axis_index("grid"), 2)
    low = 2 * ROWS * parity + HALF * parity
    copies = place_rows(far, HALF, store, low, sems)
    for copy in copies:
        copy.start()
    for copy in copies:
        copy.wait()

    def one_row(e, carry):
        i = jnp.where(parity == 0, e, ROWS - 1 - e)
        blocks = Blocks(listed, place, store, i)
        total[...] = rest[e]
        add_rows(blocks, own, i, low, total)
        finish(blocks, total, square, result.at[e])
        pltpu.make_async_copy(result.at[e], out.at[i], out_sems.at[e]).start()
        return carry

    lax.fori_loop(0, HALF, one_row, 0)
    for e in range(HALF):
        pltpu.make_async_copy(result.at[e], out.at[0], out_sems.at[e]).wait()


def local(density, pattern):
    grid = lax.axis_size("grid")
    layers = lax.axis_size("layer")
    outer_pairs = [(i, (i - 1) % grid if i % 2 == 0 else (i + 1) % grid) for i in range(grid)]
    inner_pairs = [(i, i + 1 if i % 2 == 0 else i - 1) for i in range(grid)]
    swap_pairs = []
    for y in range(layers):
        for i in range(grid):
            other = (y ^ 1) if i % 2 == 0 else ((y + 1) ^ 1) - 1
            swap_pairs.append((y * grid + i, (other % layers) * grid + i))
    inner = lax.ppermute(density, "grid", inner_pairs)
    near = lax.ppermute(pick(density, 2, True), "grid", outer_pairs)
    far = lax.ppermute(pick(density, HALF, False), "grid", outer_pairs)
    swapped = lax.ppermute(near, ("layer", "grid"), swap_pairs)
    listed, place = tables(pattern, lax.axis_index("grid"))

    store_shape = jax.ShapeDtypeStruct((LISTED * STRIDE, BS, BS), jnp.bfloat16)
    out_shape = jax.ShapeDtypeStruct((ROWS, BS, 2 * BS), jnp.float32)
    limits = pltpu.CompilerParams(vmem_limit_bytes=8 * 2**20)
    working = [
        pltpu.VMEM((BS, SPAN), jnp.float32),
        pltpu.VMEM((BS, SPAN), jnp.bfloat16),
        pltpu.VMEM((HALF, BS, 2 * BS), jnp.float32),
    ]
    store, partial = pl.pallas_call(
        close_kernel,
        out_shape=(store_shape, jax.ShapeDtypeStruct((ROWS, BS, SPAN), jnp.float32)),
        in_specs=[SMEM, SMEM, VMEM, VMEM],
        out_specs=(VMEM, VMEM),
        scratch_shapes=[pltpu.SemaphoreType.DMA((2, LISTED))],
        compiler_params=limits,
        cost_estimate=pl.CostEstimate(flops=4_000_000_000, bytes_accessed=8_000_000, transcendentals=0),
        name="close",
    )(listed, place, density, inner)
    store, rest, out = pl.pallas_call(
        near_kernel,
        out_shape=(store_shape, jax.ShapeDtypeStruct((HALF, BS, SPAN), jnp.float32), out_shape),
        in_specs=[SMEM, SMEM, VMEM, VMEM, VMEM, VMEM, VMEM],
        out_specs=(VMEM, VMEM, ANY),
        scratch_shapes=working
        + [pltpu.SemaphoreType.DMA((2, LISTED)), pltpu.SemaphoreType.DMA((HALF,))],
        input_output_aliases={6: 0},
        compiler_params=limits,
        cost_estimate=pl.CostEstimate(flops=2_000_000_000, bytes_accessed=4_000_000, transcendentals=0),
        name="near",
    )(listed, place, density, near, swapped, partial, store)
    return pl.pallas_call(
        far_kernel,
        out_shape=(store_shape, out_shape),
        in_specs=[SMEM, SMEM, VMEM, VMEM, VMEM, VMEM, ANY],
        out_specs=(VMEM, ANY),
        scratch_shapes=working
        + [pltpu.SemaphoreType.DMA((LISTED,)), pltpu.SemaphoreType.DMA((HALF,))],
        input_output_aliases={5: 0, 6: 1},
        compiler_params=limits,
        cost_estimate=pl.CostEstimate(flops=1_000_000_000, bytes_accessed=4_000_000, transcendentals=0),
        name="far",
    )(listed, place, density, far, rest, store, out)[1]


def solution(mesh):
    placed = (P("grid", None, None), P())
    return jax.shard_map(
        local, mesh=mesh, in_specs=placed, out_specs=P("grid", None, "layer"), check_vma=False
    )
```

```python
import jax
import jax.numpy as jnp
import numpy as np
from jax import lax
from jax.experimental import pallas as pl
from jax.experimental.pallas import tpu as pltpu
from jax.sharding import PartitionSpec as P

ROWS = 8
LISTED = 8
BS = 128
SPAN = LISTED * BS
WINDOW = 3 * ROWS
FAR = 4
NEAR = ROWS - FAR
SHARE = NEAR * LISTED // 2
INNER_AT = ROWS * LISTED
NEAR_AT = 2 * ROWS * LISTED
FAR_AT = NEAR_AT + NEAR * LISTED
ZERO = FAR_AT + FAR * LISTED
STORE = ZERO + 1

ANY = pl.BlockSpec(memory_space=pl.ANY)
HBM = pl.BlockSpec(memory_space=pltpu.HBM)
SMEM = pl.BlockSpec(memory_space=pltpu.SMEM)
VMEM = pl.BlockSpec(memory_space=pltpu.VMEM)


def places(odd):
    rows = []
    for w in range(FAR):
        rows.append([FAR_AT + w * LISTED + s for s in range(LISTED)])
    for w in range(FAR, ROWS):
        rows.append([NEAR_AT + (w - FAR) * LISTED + s for s in range(LISTED)])
    for base in (0, INNER_AT):
        for e in range(ROWS):
            i = ROWS - 1 - e if odd else e
            rows.append([base + s * ROWS + i for s in range(LISTED)])
    rows.append([ZERO] * LISTED)
    return np.array(rows, np.int32)


def tables(pattern):
    blocks = pattern.shape[0]
    g = lax.axis_index("grid")
    odd = g % 2 == 1
    first = g * ROWS - ROWS
    ring = jnp.concatenate([pattern[-ROWS:], pattern, pattern[:ROWS]], axis=0)
    columns = lax.dynamic_slice_in_dim(ring, g * ROWS, WINDOW, 0) - first
    columns = jnp.where(columns >= blocks, columns - blocks, columns)
    columns = jnp.where(columns < 0, columns + blocks, columns)
    columns = jnp.where(odd, WINDOW - 1 - columns[::-1], columns)
    listed = columns[ROWS : 2 * ROWS]
    columns = jnp.concatenate([columns, jnp.full((1, LISTED), -1, jnp.int32)], axis=0)
    at = jnp.where(odd, places(True), places(False))
    xs = lax.broadcasted_iota(jnp.int32, (WINDOW + 1, WINDOW), 1)
    place = jnp.full((WINDOW + 1, WINDOW), ZERO, jnp.int32)
    for s in range(LISTED):
        place = jnp.where(columns[:, s : s + 1] == xs, at[:, s : s + 1], place)
    return listed.reshape(-1), place.reshape(-1)


def parity():
    return lax.rem(lax.axis_index("grid"), 2)


def half():
    return lax.rem(lax.axis_index("layer"), 2)


def row_of(e):
    return jnp.where(parity() == 0, e, ROWS - 1 - e)


def sent_row(w):
    return jnp.where(parity() == 1, w, ROWS - 1 - w)


def pick_kernel(source, out, sems):
    copies = []
    for n in range(SHARE):
        row = sent_row(FAR + (NEAR // 2) * half() + n // LISTED)
        block = source.at[row, :, pl.ds(n % LISTED * BS, BS)]
        copies.append(pltpu.make_async_copy(block, out.at[n], sems.at[n]))
    for copy in copies:
        copy.start()
    for copy in copies:
        copy.wait()


def pick_far_kernel(source, out, sems):
    copies = []
    for n in range(FAR * LISTED):
        block = source.at[sent_row(n // LISTED), :, pl.ds(n % LISTED * BS, BS)]
        copies.append(pltpu.make_async_copy(block, out.at[n], sems.at[n]))
    for copy in copies:
        copy.start()
    for copy in copies:
        copy.wait()


class Blocks:
    def __init__(self, listed, place, store, e):
        self.listed, self.place, self.store, self.e = listed, place, store, e

    def row(self, c):
        return self.listed[self.e * LISTED + c]

    def block(self, row, a):
        return self.store[self.place[row * WINDOW + self.row(a)]]

    def pair(self, row, a):
        return jnp.concatenate([self.block(row, a), self.block(row, a + 1)], axis=1)

    def tile(self, row0, row1, a):
        return jnp.concatenate([self.pair(row0, a), self.pair(row1, a)], axis=0)

    def times(self, left, rows, a):
        total = jnp.zeros((BS, 2 * BS), jnp.float32)
        for c in range(0, LISTED, 2):
            right = self.tile(rows[c], rows[c + 1], a)
            total += jnp.dot(left(c), right, preferred_element_type=jnp.float32)
        return total


def close_rows(listed, place, own, store, partial, first):
    def one_row(n, carry):
        e = first + n
        blocks = Blocks(listed, place, store, e)
        i = row_of(e)
        rows = []
        for c in range(LISTED):
            row = blocks.row(c)
            rows.append(jnp.where(row < ROWS, WINDOW, row))
        for a in range(0, LISTED, 2):
            partial[n, :, a * BS : (a + 2) * BS] = blocks.times(
                lambda c: own[i, :, c * BS : (c + 2) * BS], rows, a
            )
        return carry

    lax.fori_loop(0, ROWS // 2, one_row, 0)


def close_kernel(listed, place, own, inner, store, partial):
    for n, source in enumerate((own, inner)):
        for r in range(ROWS):
            for s in range(LISTED):
                store[n * INNER_AT + s * ROWS + r] = source[r, :, s * BS : (s + 1) * BS]
    store[ZERO] = jnp.zeros((BS, BS), jnp.bfloat16)
    close_rows(listed, place, own, store, partial, 0)


def close_kernel2(listed, place, own, store, partial):
    close_rows(listed, place, own, store, partial, ROWS // 2)


def chosen(blocks, low, high, index, most):
    base = blocks.e * LISTED
    for t in range(LISTED):
        index[base + t] = 0
    count = jnp.int32(0)
    for c in range(LISTED):
        row = blocks.row(c)
        index[base + count] = c
        count += jnp.logical_and(row >= low, row < high).astype(jnp.int32)
    picks = []
    for t in range(most):
        valid = t < count
        c = jnp.where(valid, index[base + t], 0)
        picks.append((c, jnp.where(valid, blocks.row(c), WINDOW)))
    return count, picks


def step(blocks, own, picks, a):
    i = row_of(blocks.e)
    left = jnp.concatenate(
        [own[i, :, pl.ds(pl.multiple_of(c * BS, BS), BS)] for c, _ in picks], axis=1
    )
    right = blocks.tile(picks[0][1], picks[1][1], a)
    return jnp.dot(left, right, preferred_element_type=jnp.float32)


def add_rows(listed, place, store, own, source, total, rows, low, high, mosts, index):
    later = []
    for e, most in zip(rows, mosts):
        blocks = Blocks(listed, place, store, e)
        count, picks = chosen(blocks, low, high, index, most)
        for a in range(0, LISTED, 2):
            cols = slice(a * BS, (a + 2) * BS)
            total[e - rows[0], :, cols] = source(e)[:, cols] + step(blocks, own, picks[:2], a)
        for t in range(2, most, 2):
            later.append((blocks, count, picks[t : t + 2], t))
    for blocks, count, picks, t in later:

        @pl.when(count > t)
        def _():
            for a in range(0, LISTED, 2):
                cols = slice(a * BS, (a + 2) * BS)
                total[blocks.e - rows[0], :, cols] += step(blocks, own, picks, a)


def finish(listed, place, store, total, rows, square, result, out, sems):
    layer = lax.axis_index("layer")
    start = pl.multiple_of(layer * 2 * BS, 2 * BS)
    copies = []
    for e in rows:
        n = e - rows[0]
        blocks = Blocks(listed, place, store, e)
        square[n] = total[n].astype(jnp.bfloat16)
        cube = blocks.times(
            lambda c: square[n, :, c * BS : (c + 2) * BS],
            [blocks.row(c) for c in range(LISTED)],
            2 * layer,
        )
        result[n] = 3.0 * square[n, :, pl.ds(start, 2 * BS)].astype(jnp.float32) - 2.0 * cube
        copies.append(pltpu.make_async_copy(result.at[n], out.at[row_of(e)], sems.at[n]))
        copies[-1].start()
    for copy in copies:
        copy.wait()


def insert(pieces, store, sems):
    copies = [
        pltpu.make_async_copy(piece, store.at[pl.ds(at, count)], sems.at[n])
        for n, (piece, at, count) in enumerate(pieces)
    ]
    for copy in copies:
        copy.start()
    for copy in copies:
        copy.wait()


def share_low(mine):
    return FAR + NEAR // 2 * (half() if mine else 1 - half())


def near_kernel(listed, place, own, near, partial, partial2, _, store, sums, index, sems):
    insert([(near, NEAR_AT + SHARE * half(), SHARE)], store, sems)
    low = share_low(True)
    source = lambda e: partial.at[e] if e < ROWS // 2 else partial2.at[e - ROWS // 2]
    add_rows(
        listed, place, store, own, source, sums, list(range(ROWS)), low, low + 2, [2] * ROWS, index
    )


def swapped_kernel(
    listed, place, own, swapped, sums, _, store, rest, out, total, square, result, index, sems, out_sems
):
    insert([(swapped, NEAR_AT + SHARE * (1 - half()), SHARE)], store, sems)
    low = share_low(False)
    source = lambda e: sums.at[e]
    ended, left = list(range(FAR, ROWS)), list(range(FAR))
    add_rows(listed, place, store, own, source, total, ended, low, low + 2, [2] * NEAR, index)
    add_rows(listed, place, store, own, source, rest, left, low, low + 2, [2] * FAR, index)
    finish(listed, place, store, total, ended, square, result, out, out_sems)


def far_kernel(
    listed, place, own, far, rest, _s, _o, store, out, total, square, result, index, sems, out_sems
):
    insert([(far, FAR_AT, FAR * LISTED)], store, sems)
    source = lambda e: rest.at[e]
    rows = list(range(FAR))
    add_rows(listed, place, store, own, source, total, rows, 0, FAR, [4, 4, 2, 2], index)
    finish(listed, place, store, total, rows, square, result, out, out_sems)


def shape(*dims, dtype=jnp.bfloat16):
    return jax.ShapeDtypeStruct(dims, dtype)


def cost(flops):
    return pl.CostEstimate(flops=flops, bytes_accessed=4_000_000, transcendentals=0)


def local(density, pattern):
    grid = lax.axis_size("grid")
    layers = lax.axis_size("layer")
    outer_pairs = [(i, (i - 1) % grid if i % 2 == 0 else (i + 1) % grid) for i in range(grid)]
    inner_pairs = [(i, i + 1 if i % 2 == 0 else i - 1) for i in range(grid)]
    swap_pairs = []
    for y in range(layers):
        for i in range(grid):
            other = (y ^ 1) if i % 2 == 0 else ((y + 1) ^ 1) - 1
            swap_pairs.append((y * grid + i, (other % layers) * grid + i))
    small = pltpu.CompilerParams(vmem_limit_bytes=8 * 2**20)
    limits = pltpu.CompilerParams(vmem_limit_bytes=24 * 2**20)

    def pick(kernel, count, source, name):
        return pl.pallas_call(
            kernel,
            out_shape=pltpu.VMEM((count, BS, BS), jnp.bfloat16),
            in_specs=[HBM],
            out_specs=VMEM,
            scratch_shapes=[pltpu.SemaphoreType.DMA((count,))],
            compiler_params=small,
            name=name,
        )(pltpu.with_memory_space_constraint(source, pltpu.HBM))

    picked = pick(pick_kernel, SHARE, density, "pick")
    density, picked = lax.optimization_barrier((density, picked))
    inner = lax.ppermute(density, "grid", inner_pairs)
    near = lax.ppermute(picked, "grid", outer_pairs)
    far = lax.ppermute(pick(pick_far_kernel, FAR * LISTED, density, "pick_far"), "grid", outer_pairs)

    listed, place = tables(pattern)
    store_shape = shape(STORE, BS, BS)
    out_shape = shape(ROWS, BS, 2 * BS, dtype=jnp.float32)

    def working(rows):
        return [
            pltpu.VMEM((rows, BS, SPAN), jnp.float32),
            pltpu.VMEM((rows, BS, SPAN), jnp.bfloat16),
            pltpu.VMEM((rows, BS, 2 * BS), jnp.float32),
            pltpu.SMEM((ROWS * LISTED,), jnp.int32),
            pltpu.SemaphoreType.DMA((2,)),
            pltpu.SemaphoreType.DMA((rows,)),
        ]

    half_shape = shape(ROWS // 2, BS, SPAN, dtype=jnp.float32)
    store, partial = pl.pallas_call(
        close_kernel,
        out_shape=(store_shape, half_shape),
        in_specs=[SMEM, SMEM, VMEM, VMEM],
        out_specs=(VMEM, VMEM),
        compiler_params=limits,
        cost_estimate=cost(2_000_000_000),
        name="close",
    )(listed, place, density, inner)
    near, partial = lax.optimization_barrier((near, partial))
    swapped = lax.ppermute(near, ("layer", "grid"), swap_pairs)
    partial2 = pl.pallas_call(
        close_kernel2,
        out_shape=half_shape,
        in_specs=[SMEM, SMEM, VMEM, VMEM],
        out_specs=VMEM,
        compiler_params=limits,
        cost_estimate=cost(2_000_000_000),
        name="close2",
    )(listed, place, density, store)
    store, sums = pl.pallas_call(
        near_kernel,
        out_shape=(store_shape, shape(ROWS, BS, SPAN, dtype=jnp.float32)),
        in_specs=[SMEM, SMEM] + [VMEM] * 5,
        out_specs=(VMEM, VMEM),
        scratch_shapes=[pltpu.SMEM((ROWS * LISTED,), jnp.int32), pltpu.SemaphoreType.DMA((1,))],
        input_output_aliases={6: 0},
        compiler_params=limits,
        cost_estimate=cost(2_000_000_000),
        name="near",
    )(listed, place, density, near, partial, partial2, store)
    store, rest, out = pl.pallas_call(
        swapped_kernel,
        out_shape=(store_shape, shape(FAR, BS, SPAN, dtype=jnp.float32), out_shape),
        in_specs=[SMEM, SMEM] + [VMEM] * 4,
        out_specs=(VMEM, VMEM, ANY),
        scratch_shapes=working(NEAR),
        input_output_aliases={5: 0},
        compiler_params=limits,
        cost_estimate=cost(2_000_000_000),
        name="swapped",
    )(listed, place, density, swapped, sums, store)
    return pl.pallas_call(
        far_kernel,
        out_shape=(store_shape, out_shape),
        in_specs=[SMEM, SMEM] + [VMEM] * 4 + [ANY],
        out_specs=(VMEM, ANY),
        scratch_shapes=working(FAR),
        input_output_aliases={5: 0, 6: 1},
        compiler_params=limits,
        cost_estimate=cost(2_000_000_000),
        name="far",
    )(listed, place, density, far, rest, store, out)[1]


def solution(mesh):
    placed = (P("grid", None, None), P())
    return jax.shard_map(
        local, mesh=mesh, in_specs=placed, out_specs=P("grid", None, "layer"), check_vma=False
    )
```

```python
import jax
import jax.numpy as jnp
import numpy as np
from jax import lax
from jax.experimental import pallas as pl
from jax.experimental.pallas import tpu as pltpu
from jax.sharding import PartitionSpec as P

ROWS = 8
LISTED = 8
BS = 128
SPAN = LISTED * BS
WINDOW = 3 * ROWS
FAR = 5
NEAR = ROWS - FAR
SHARE = NEAR * LISTED // 2
FAR_BLOCKS = FAR * LISTED
FIRST = 28
REST = FAR_BLOCKS - FIRST
EARLY_EVERY = 16
INNER_AT = ROWS * LISTED
NEAR_AT = 2 * ROWS * LISTED
FAR_AT = NEAR_AT + 2 * SHARE
ZERO = FAR_AT + FAR_BLOCKS
STORE = ZERO + 1

ANY = pl.BlockSpec(memory_space=pl.ANY)
HBM = pl.BlockSpec(memory_space=pltpu.HBM)
SMEM = pl.BlockSpec(memory_space=pltpu.SMEM)
VMEM = pl.BlockSpec(memory_space=pltpu.VMEM)


def places(odd):
    middle = LISTED // 2
    rows = [
        [NEAR_AT + s for s in range(LISTED)],
        [NEAR_AT + LISTED + s + (SHARE - middle if s >= middle else 0) for s in range(LISTED)],
        [NEAR_AT + SHARE + s for s in range(LISTED)],
    ]
    for base in (0, INNER_AT):
        for e in range(ROWS):
            i = ROWS - 1 - e if odd else e
            rows.append([base + s * ROWS + i for s in range(LISTED)])
    rows.append([ZERO] * LISTED)
    return np.array(rows, np.int32)


def tables(pattern, far_places):
    blocks = pattern.shape[0]
    g = lax.axis_index("grid")
    odd = g % 2 == 1
    first = g * ROWS - ROWS
    ring = jnp.concatenate([pattern[-ROWS:], pattern, pattern[:ROWS]], axis=0)
    columns = lax.dynamic_slice_in_dim(ring, g * ROWS, WINDOW, 0) - first
    columns = jnp.where(columns >= blocks, columns - blocks, columns)
    columns = jnp.where(columns < 0, columns + blocks, columns)
    columns = jnp.where(odd, WINDOW - 1 - columns[::-1], columns)
    listed = columns[ROWS : 2 * ROWS]
    columns = jnp.concatenate([columns, jnp.full((1, LISTED), -1, jnp.int32)], axis=0)
    at = jnp.where(odd, places(True), places(False))
    at = jnp.concatenate([far_places.reshape(FAR, LISTED), at], axis=0)
    xs = lax.broadcasted_iota(jnp.int32, (WINDOW + 1, WINDOW), 1)
    place = jnp.full((WINDOW + 1, WINDOW), ZERO, jnp.int32)
    for s in range(LISTED):
        place = jnp.where(columns[:, s : s + 1] == xs, at[:, s : s + 1], place)
    return listed.reshape(-1), place.reshape(-1)


def ones(bits):
    bits = (bits & 0x55555555) + ((bits >> 1) & 0x55555555)
    bits = (bits & 0x33333333) + ((bits >> 2) & 0x33333333)
    bits = (bits & 0x0F0F0F0F) + ((bits >> 4) & 0x0F0F0F0F)
    bits = bits + (bits >> 8)
    return (bits + (bits >> 16)) & 0xFF


def positions(pattern):
    blocks = pattern.shape[1]
    row = lax.broadcasted_iota(jnp.int32, pattern.shape, 1)
    slot = lax.broadcasted_iota(jnp.int32, pattern.shape, 0)
    offset = pattern - row + ROWS
    offset = jnp.where(offset < 0, offset + blocks, offset)
    offset = jnp.where(offset >= blocks, offset - blocks, offset)
    bits = jnp.sum(jnp.left_shift(1, offset), axis=0, keepdims=True)
    bits = jnp.broadcast_to(bits, pattern.shape)
    k = row & (ROWS - 1)
    forward = (row & ROWS) != 0
    uses = jnp.zeros(pattern.shape, jnp.int32)
    for d in range(1, ROWS + 1):
        after = pltpu.roll(bits, blocks - d, 1)
        before = pltpu.roll(bits, d, 1)
        hit_after = jnp.logical_and(k + d >= ROWS, ((after >> (ROWS - d)) & 1) == 1)
        hit_before = jnp.logical_and(k - d < 0, ((before >> (ROWS + d)) & 1) == 1)
        uses = uses | jnp.where(
            forward, jnp.where(hit_after, after << d, 0), jnp.where(hit_before, before >> d, 0)
        )
    far = jnp.where(forward, k, ROWS - 1 - k) < FAR
    mask = jnp.where(far, bits & uses, 0)
    sent = (mask >> offset) & 1
    up_to = sent
    for d in (1, 2, 4):
        up_to = up_to + jnp.where(slot >= d, pltpu.roll(up_to, d, 0), 0)
    count = ones(mask)
    ahead, behind = count, count
    for d in (1, 2, 4):
        ahead = ahead + jnp.where(k >= d, pltpu.roll(ahead, d, 1), 0)
        behind = behind + jnp.where(k < ROWS - d, pltpu.roll(behind, blocks - d, 1), 0)
    position = jnp.where(forward, ahead, behind) - count + up_to - sent
    most = jnp.max(ahead.astype(jnp.float32))
    return jnp.where(sent == 1, position, FAR_BLOCKS), most


def parity():
    return lax.rem(lax.axis_index("grid"), 2)


def half():
    return lax.rem(lax.axis_index("layer"), 2)


def row_of(e):
    return jnp.where(parity() == 0, e, ROWS - 1 - e)


def sent_row(w):
    return jnp.where(parity() == 1, w, ROWS - 1 - w)


def pick_kernel(source, pattern, out, moves, flag, listed, sems):
    whole = sent_row(FAR + 2 * half())
    start = pl.multiple_of(half() * (SPAN // 2), SPAN // 2)
    copies = [
        pltpu.make_async_copy(pattern, listed, sems.at[0]),
        pltpu.make_async_copy(source.at[whole], out.at[:, pl.ds(0, SPAN)], sems.at[1]),
        pltpu.make_async_copy(
            source.at[sent_row(FAR + 1), :, pl.ds(start, SPAN // 2)], out.at[:, pl.ds(SPAN, SPAN // 2)], sems.at[2]
        ),
    ]
    for copy in copies:
        copy.start()
    copies[0].wait()
    position, most = positions(listed[...])
    blocks = pattern.shape[1]
    shift = blocks - ROWS * lax.rem(lax.axis_index("grid") + lax.axis_size("grid") - 1, lax.axis_size("grid"))
    moves[...] = pltpu.roll(position, lax.rem(shift, blocks), 1)[:, :BS]
    flag[0] = (most > FIRST).astype(jnp.int32)
    for copy in copies[1:]:
        copy.wait()


def waits_long():
    return lax.rem(lax.axis_index("grid"), EARLY_EVERY) == 0


def pack(moves, source, own, packed, sems):
    start = jnp.where(parity() == 1, 0, ROWS - FAR)
    rows = pltpu.make_async_copy(source.at[pl.ds(start, FAR)], own, sems.at[1])
    rows.start()
    rows.wait()
    for k in range(FAR):
        held = jnp.where(parity() == 1, k, FAR - 1 - k)
        for s in range(LISTED):
            packed[moves[s, ROWS + sent_row(k)]] = own[held, :, s * BS : (s + 1) * BS]


def pack_first(moves, source, first, own, packed, sems):
    pack(moves, source, own, packed, sems)
    copy = pltpu.make_async_copy(packed.at[pl.ds(0, FIRST)], first, sems.at[0])
    copy.start()
    copy.wait()


def early_pack_kernel(moves, source, first, unused, *scratch):
    @pl.when(waits_long())
    def _():
        pack_first(moves, source, first, *scratch)


def late_pack_kernel(moves, source, _, first, far_places, *scratch):
    for k in range(FAR):
        row = jnp.where(parity() == 0, k, WINDOW - 1 - k)
        for s in range(LISTED):
            place = moves[s, row]
            far_places[k * LISTED + s] = jnp.where(place == FAR_BLOCKS, ZERO, FAR_AT + place)

    @pl.when(jnp.logical_not(waits_long()))
    def _():
        pack_first(moves, source, first, *scratch)


def pack_rest_kernel(moves, source, rest, own, packed, sems):
    pack(moves, source, own, packed, sems)
    copy = pltpu.make_async_copy(packed.at[pl.ds(FIRST, REST)], rest, sems.at[0])
    copy.start()
    copy.wait()


class Blocks:
    def __init__(self, listed, place, store, e):
        self.listed, self.place, self.store, self.e = listed, place, store, e

    def row(self, c):
        return self.listed[self.e * LISTED + c]

    def block(self, row, a):
        return self.store[self.place[row * WINDOW + self.row(a)]]

    def pair(self, row, a):
        return jnp.concatenate([self.block(row, a), self.block(row, a + 1)], axis=1)

    def tile(self, row0, row1, a):
        return jnp.concatenate([self.pair(row0, a), self.pair(row1, a)], axis=0)

    def times(self, left, rows, a):
        total = jnp.zeros((BS, 2 * BS), jnp.float32)
        for c in range(0, LISTED, 2):
            right = self.tile(rows[c], rows[c + 1], a)
            total += jnp.dot(left(c), right, preferred_element_type=jnp.float32)
        return total


def close_kernel(listed, place, own, inner, near, store, partial):
    for n, source in enumerate((own, inner)):
        for r in range(ROWS):
            for s in range(LISTED):
                store[n * INNER_AT + s * ROWS + r] = source[r, :, s * BS : (s + 1) * BS]
    place_share(near, store, True)
    store[ZERO] = jnp.zeros((BS, BS), jnp.bfloat16)
    whole = FAR + 2 * half()

    def one_row(e, carry):
        blocks = Blocks(listed, place, store, e)
        i = row_of(e)
        rows = []
        for c in range(LISTED):
            row = blocks.row(c)
            away = jnp.logical_and(row < ROWS, row != whole)
            rows.append(jnp.where(away, WINDOW, row))
        for a in range(0, LISTED, 2):
            partial[e, :, a * BS : (a + 2) * BS] = blocks.times(
                lambda c: own[i, :, c * BS : (c + 2) * BS], rows, a
            )
        return carry

    lax.fori_loop(0, ROWS, one_row, 0)


def chosen(blocks, low, high, index, most):
    base = blocks.e * LISTED
    for t in range(LISTED):
        index[base + t] = 0
    count = jnp.int32(0)
    for c in range(LISTED):
        row = blocks.row(c)
        index[base + count] = c
        count += jnp.logical_and(row >= low, row < high).astype(jnp.int32)
    picks = []
    for t in range(most):
        valid = t < count
        c = jnp.where(valid, index[base + t], 0)
        picks.append((c, jnp.where(valid, blocks.row(c), WINDOW)))
    return count, picks


def step(blocks, own, picks, a):
    i = row_of(blocks.e)
    left = jnp.concatenate(
        [own[i, :, pl.ds(pl.multiple_of(c * BS, BS), BS)] for c, _ in picks], axis=1
    )
    right = blocks.tile(picks[0][1], picks[1][1], a)
    return jnp.dot(left, right, preferred_element_type=jnp.float32)


def add_rows(listed, place, store, own, source, total, rows, low, high, mosts, index):
    later = []
    for e, most in zip(rows, mosts):
        blocks = Blocks(listed, place, store, e)
        count, picks = chosen(blocks, low, high, index, most)
        for a in range(0, LISTED, 2):
            cols = slice(a * BS, (a + 2) * BS)
            total[e - rows[0], :, cols] = source(e)[:, cols] + step(blocks, own, picks[:2], a)
        for t in range(2, most, 2):
            later.append((blocks, count, picks[t : t + 2], t))
    for blocks, count, picks, t in later:

        @pl.when(count > t)
        def _():
            for a in range(0, LISTED, 2):
                cols = slice(a * BS, (a + 2) * BS)
                total[blocks.e - rows[0], :, cols] += step(blocks, own, picks, a)


def finish(listed, place, store, total, rows, square, result, out, sems):
    layer = lax.axis_index("layer")
    start = pl.multiple_of(layer * 2 * BS, 2 * BS)
    copies = []
    for e in rows:
        n = e - rows[0]
        blocks = Blocks(listed, place, store, e)
        square[n] = total[n].astype(jnp.bfloat16)
        cube = blocks.times(
            lambda c: square[n, :, c * BS : (c + 2) * BS],
            [blocks.row(c) for c in range(LISTED)],
            2 * layer,
        )
        result[n] = 3.0 * square[n, :, pl.ds(start, 2 * BS)].astype(jnp.float32) - 2.0 * cube
        copies.append(pltpu.make_async_copy(result.at[n], out.at[row_of(e)], sems.at[n]))
        copies[-1].start()
    for copy in copies:
        copy.wait()


def insert(pieces, store, sems):
    copies = [
        pltpu.make_async_copy(piece, store.at[pl.ds(at, count)], sems.at[n])
        for n, (piece, at, count) in enumerate(pieces)
    ]
    for copy in copies:
        copy.start()
    for copy in copies:
        copy.wait()


def place_share(share, store, mine):
    base = NEAR_AT + SHARE * (half() if mine else 1 - half())
    for n in range(SHARE):
        store[base + n] = share[:, n * BS : (n + 1) * BS]


def swapped_kernel(
    listed, place, own, swapped, sums, _, store, rest, out, total, square, result, index, out_sems
):
    place_share(swapped, store, False)
    low = FAR + 1 - half()
    source = lambda e: sums.at[e]
    ended, left = list(range(FAR, ROWS)), list(range(FAR))
    add_rows(listed, place, store, own, source, total, ended, low, low + 2, [2] * NEAR, index)
    add_rows(listed, place, store, own, source, rest, left, low, low + 2, [2] * FAR, index)
    finish(listed, place, store, total, ended, square, result, out, out_sems)


def far_kernel(
    listed, place, own, first, last, rest, _s, _o, store, out, total, square, result, index, out_sems, sems
):
    insert([(first, FAR_AT, FIRST), (last, FAR_AT + FIRST, REST)], store, sems)
    source = lambda e: rest.at[e]
    rows = list(range(FAR))
    add_rows(listed, place, store, own, source, total, rows, 0, FAR, [6, 4, 4, 2, 2], index)
    finish(listed, place, store, total, rows, square, result, out, out_sems)


def shape(*dims, dtype=jnp.bfloat16):
    return jax.ShapeDtypeStruct(dims, dtype)


def cost(flops):
    return pl.CostEstimate(flops=flops, bytes_accessed=4_000_000, transcendentals=0)


def local(density, pattern):
    grid = lax.axis_size("grid")
    layers = lax.axis_size("layer")
    outer_pairs = [(i, (i - 1) % grid if i % 2 == 0 else (i + 1) % grid) for i in range(grid)]
    inner_pairs = [(i, i + 1 if i % 2 == 0 else i - 1) for i in range(grid)]
    swap_pairs = []
    for y in range(layers):
        for i in range(grid):
            other = (y ^ 1) if i % 2 == 0 else ((y + 1) ^ 1) - 1
            swap_pairs.append((y * grid + i, (other % layers) * grid + i))
    small = pltpu.CompilerParams(vmem_limit_bytes=8 * 2**20)
    limits = pltpu.CompilerParams(vmem_limit_bytes=24 * 2**20)

    in_hbm = pltpu.with_memory_space_constraint(density, pltpu.HBM)
    by_slot = pltpu.with_memory_space_constraint(pattern.T, pltpu.HBM)
    picked, moves, flag = pl.pallas_call(
        pick_kernel,
        out_shape=(
            shape(BS, SHARE * BS),
            jax.ShapeDtypeStruct((LISTED, BS), jnp.int32),
            jax.ShapeDtypeStruct((1,), jnp.int32),
        ),
        in_specs=[HBM, HBM],
        out_specs=(VMEM, VMEM, SMEM),
        scratch_shapes=[pltpu.VMEM(by_slot.shape, jnp.int32), pltpu.SemaphoreType.DMA((3,))],
        compiler_params=small,
        name="pick",
    )(in_hbm, by_slot)
    inner_sent, picked = lax.optimization_barrier((density, picked))
    inner = lax.ppermute(inner_sent, "grid", inner_pairs)
    packing = dict(
        scratch_shapes=[
            pltpu.VMEM((FAR, BS, SPAN), jnp.bfloat16),
            pltpu.VMEM((FAR_BLOCKS + 1, BS, BS), jnp.bfloat16),
            pltpu.SemaphoreType.DMA((2,)),
        ],
        compiler_params=small,
    )
    first, unused = pl.pallas_call(
        early_pack_kernel,
        out_shape=(shape(FIRST, BS, BS), shape(REST, BS, BS)),
        in_specs=[SMEM, HBM],
        out_specs=(ANY, ANY),
        name="early_pack",
        **packing,
    )(moves, in_hbm)
    picked, first = lax.optimization_barrier((picked, first))
    near = lax.ppermute(picked, "grid", outer_pairs)
    first, far_places = pl.pallas_call(
        late_pack_kernel,
        out_shape=(shape(FIRST, BS, BS), jax.ShapeDtypeStruct((FAR_BLOCKS,), jnp.int32)),
        in_specs=[SMEM, HBM, ANY],
        out_specs=(ANY, SMEM),
        input_output_aliases={2: 0},
        name="late_pack",
        **packing,
    )(moves, in_hbm, first)
    first = lax.ppermute(first, "grid", outer_pairs)

    def send_rest(_):
        rest = pl.pallas_call(
            pack_rest_kernel,
            out_shape=shape(REST, BS, BS),
            in_specs=[SMEM, HBM],
            out_specs=ANY,
            name="pack_rest",
            **packing,
        )(moves, in_hbm)
        return lax.ppermute(rest, "grid", outer_pairs)

    last = lax.cond(flag[0] > 0, send_rest, lambda blocks: blocks, unused)

    listed, place = tables(pattern, far_places)
    listed, last = lax.optimization_barrier((listed, last))
    store_shape = shape(STORE, BS, BS)
    out_shape = shape(ROWS, BS, 2 * BS, dtype=jnp.float32)

    def working(rows):
        return [
            pltpu.VMEM((rows, BS, SPAN), jnp.float32),
            pltpu.VMEM((rows, BS, SPAN), jnp.bfloat16),
            pltpu.VMEM((rows, BS, 2 * BS), jnp.float32),
            pltpu.SMEM((ROWS * LISTED,), jnp.int32),
            pltpu.SemaphoreType.DMA((rows,)),
        ]

    swapped = lax.ppermute(near, ("layer", "grid"), swap_pairs)
    store, sums = pl.pallas_call(
        close_kernel,
        out_shape=(store_shape, shape(ROWS, BS, SPAN, dtype=jnp.float32)),
        in_specs=[SMEM, SMEM, VMEM, VMEM, VMEM],
        out_specs=(VMEM, VMEM),
        compiler_params=limits,
        cost_estimate=cost(4_000_000_000),
        name="close",
    )(listed, place, density, inner, near)
    store, rest, out = pl.pallas_call(
        swapped_kernel,
        out_shape=(store_shape, shape(FAR, BS, SPAN, dtype=jnp.float32), out_shape),
        in_specs=[SMEM, SMEM] + [VMEM] * 4,
        out_specs=(VMEM, VMEM, ANY),
        scratch_shapes=working(NEAR),
        input_output_aliases={5: 0},
        compiler_params=limits,
        cost_estimate=cost(2_000_000_000),
        name="swapped",
    )(listed, place, density, swapped, sums, store)
    return pl.pallas_call(
        far_kernel,
        out_shape=(store_shape, out_shape),
        in_specs=[SMEM, SMEM] + [VMEM] * 5 + [ANY],
        out_specs=(VMEM, ANY),
        scratch_shapes=working(FAR) + [pltpu.SemaphoreType.DMA((2,))],
        input_output_aliases={6: 0, 7: 1},
        compiler_params=limits,
        cost_estimate=cost(2_000_000_000),
        name="far",
    )(listed, place, density, first, last, rest, store, out)[1]


def solution(mesh):
    placed = (P("grid", None, None), P())
    return jax.shard_map(
        local, mesh=mesh, in_specs=placed, out_specs=P("grid", None, "layer"), check_vma=False
    )
```

```python
import jax
import jax.numpy as jnp
import numpy as np
from jax import lax
from jax.experimental import pallas as pl
from jax.experimental.pallas import tpu as pltpu
from jax.sharding import PartitionSpec as P

ROWS = 8
LISTED = 8
BS = 128
SPAN = LISTED * BS
WINDOW = 3 * ROWS
FAR = 5
NEAR = ROWS - FAR
SHARE = NEAR * LISTED // 2
FAR_BLOCKS = FAR * LISTED
FIRST = 28
REST = FAR_BLOCKS - FIRST
EARLY_EVERY = 16
INNER_AT = ROWS * LISTED
NEAR_AT = 2 * ROWS * LISTED
FAR_AT = NEAR_AT + 2 * SHARE
ZERO = FAR_AT + FAR_BLOCKS
STORE = ZERO + 1

ANY = pl.BlockSpec(memory_space=pl.ANY)
HBM = pl.BlockSpec(memory_space=pltpu.HBM)
SMEM = pl.BlockSpec(memory_space=pltpu.SMEM)
VMEM = pl.BlockSpec(memory_space=pltpu.VMEM)


def places(odd):
    middle = LISTED // 2
    rows = [
        [NEAR_AT + s for s in range(LISTED)],
        [NEAR_AT + LISTED + s + (SHARE - middle if s >= middle else 0) for s in range(LISTED)],
        [NEAR_AT + SHARE + s for s in range(LISTED)],
    ]
    for base in (0, INNER_AT):
        for e in range(ROWS):
            i = ROWS - 1 - e if odd else e
            rows.append([base + s * ROWS + i for s in range(LISTED)])
    rows.append([ZERO] * LISTED)
    return np.array(rows, np.int32)


def tables(pattern, moves):
    blocks = pattern.shape[0]
    g = lax.axis_index("grid")
    odd = g % 2 == 1
    first = g * ROWS - ROWS
    ring = jnp.concatenate([pattern[-ROWS:], pattern, pattern[:ROWS]], axis=0)
    columns = lax.dynamic_slice_in_dim(ring, g * ROWS, WINDOW, 0) - first
    columns = jnp.where(columns >= blocks, columns - blocks, columns)
    columns = jnp.where(columns < 0, columns + blocks, columns)
    columns = jnp.where(odd, WINDOW - 1 - columns[::-1], columns)
    listed = columns[ROWS : 2 * ROWS]
    columns = jnp.concatenate([columns, jnp.full((1, LISTED), -1, jnp.int32)], axis=0)
    at = jnp.where(odd, places(True), places(False))
    far = jnp.where(odd, moves[:, WINDOW - FAR : WINDOW][:, ::-1], moves[:, :FAR]).T
    far = jnp.where(far == FAR_BLOCKS, ZERO, FAR_AT + far)
    at = jnp.concatenate([far, at], axis=0)
    xs = lax.broadcasted_iota(jnp.int32, (WINDOW + 1, WINDOW), 1)
    place = jnp.full((WINDOW + 1, WINDOW), ZERO, jnp.int32)
    for s in range(LISTED):
        place = jnp.where(columns[:, s : s + 1] == xs, at[:, s : s + 1], place)
    return listed.reshape(-1), place.reshape(-1)


def ones(bits):
    bits = (bits & 0x55555555) + ((bits >> 1) & 0x55555555)
    bits = (bits & 0x33333333) + ((bits >> 2) & 0x33333333)
    bits = (bits & 0x0F0F0F0F) + ((bits >> 4) & 0x0F0F0F0F)
    bits = bits + (bits >> 8)
    return (bits + (bits >> 16)) & 0xFF


def positions(pattern):
    blocks = pattern.shape[1]
    row = lax.broadcasted_iota(jnp.int32, pattern.shape, 1)
    slot = lax.broadcasted_iota(jnp.int32, pattern.shape, 0)
    offset = pattern - row + ROWS
    offset = jnp.where(offset < 0, offset + blocks, offset)
    offset = jnp.where(offset >= blocks, offset - blocks, offset)
    bits = jnp.sum(jnp.left_shift(1, offset), axis=0, keepdims=True)
    bits = jnp.broadcast_to(bits, pattern.shape)
    k = row & (ROWS - 1)
    forward = (row & ROWS) != 0
    uses = jnp.zeros(pattern.shape, jnp.int32)
    for d in range(1, ROWS + 1):
        after = pltpu.roll(bits, blocks - d, 1)
        before = pltpu.roll(bits, d, 1)
        hit_after = jnp.logical_and(k + d >= ROWS, ((after >> (ROWS - d)) & 1) == 1)
        hit_before = jnp.logical_and(k - d < 0, ((before >> (ROWS + d)) & 1) == 1)
        uses = uses | jnp.where(
            forward, jnp.where(hit_after, after << d, 0), jnp.where(hit_before, before >> d, 0)
        )
    far = jnp.where(forward, k, ROWS - 1 - k) < FAR
    mask = jnp.where(far, bits & uses, 0)
    sent = (mask >> offset) & 1
    up_to = sent
    for d in (1, 2, 4):
        up_to = up_to + jnp.where(slot >= d, pltpu.roll(up_to, d, 0), 0)
    count = ones(mask)
    ahead, behind = count, count
    for d in (1, 2, 4):
        ahead = ahead + jnp.where(k >= d, pltpu.roll(ahead, d, 1), 0)
        behind = behind + jnp.where(k < ROWS - d, pltpu.roll(behind, blocks - d, 1), 0)
    position = jnp.where(forward, ahead, behind) - count + up_to - sent
    most = jnp.max(ahead.astype(jnp.float32))
    return jnp.where(sent == 1, position, FAR_BLOCKS), most


def parity():
    return lax.rem(lax.axis_index("grid"), 2)


def half():
    return lax.rem(lax.axis_index("layer"), 2)


def row_of(e):
    return jnp.where(parity() == 0, e, ROWS - 1 - e)


def sent_row(w):
    return jnp.where(parity() == 1, w, ROWS - 1 - w)


def pick_kernel(source, out, sems):
    whole = sent_row(FAR + 2 * half())
    start = pl.multiple_of(half() * (SPAN // 2), SPAN // 2)
    copies = [
        pltpu.make_async_copy(source.at[whole], out.at[:, pl.ds(0, SPAN)], sems.at[0]),
        pltpu.make_async_copy(
            source.at[sent_row(FAR + 1), :, pl.ds(start, SPAN // 2)], out.at[:, pl.ds(SPAN, SPAN // 2)], sems.at[1]
        ),
    ]
    for copy in copies:
        copy.start()
    for copy in copies:
        copy.wait()


def waits_long():
    return lax.rem(lax.axis_index("grid"), EARLY_EVERY) == 0


def pack(first, count, pattern, source, out, moves, listed, own, window, places, packed, sems):
    fetch = pltpu.make_async_copy(pattern, listed, sems.at[0])
    fetch.start()
    start = jnp.where(parity() == 1, 0, ROWS - FAR)
    rows = pltpu.make_async_copy(source.at[pl.ds(start, FAR)], own, sems.at[1])
    rows.start()
    fetch.wait()
    position, most = positions(listed[...])
    blocks, grid = pattern.shape[1], lax.axis_size("grid")
    shift = blocks - ROWS * lax.rem(lax.axis_index("grid") + grid - 1, grid)
    position = pltpu.roll(position, lax.rem(shift, blocks), 1)[:, :BS]
    lane = lax.broadcasted_iota(jnp.int32, position.shape, 1)
    window[...] = jnp.where(lane == BS - 1, (most > FIRST).astype(jnp.int32), position)
    scalars = pltpu.make_async_copy(window, places, sems.at[0])
    scalars.start()
    table = pltpu.make_async_copy(window, moves, sems.at[2])
    table.start()
    scalars.wait()
    rows.wait()
    for k in range(FAR):
        held = jnp.where(parity() == 1, k, FAR - 1 - k)
        for s in range(LISTED):
            packed[places[s, ROWS + sent_row(k)]] = own[held, :, s * BS : (s + 1) * BS]
    copy = pltpu.make_async_copy(packed.at[pl.ds(first, count)], out, sems.at[0])
    copy.start()
    copy.wait()
    table.wait()


def early_pack_kernel(pattern, source, first, moves, unused, *scratch):
    @pl.when(waits_long())
    def _():
        pack(0, FIRST, pattern, source, first, moves, *scratch)


def late_pack_kernel(pattern, source, _f, _m, first, moves, *scratch):
    @pl.when(jnp.logical_not(waits_long()))
    def _():
        pack(0, FIRST, pattern, source, first, moves, *scratch)


def pack_rest_kernel(*refs):
    pack(FIRST, REST, *refs)


class Blocks:
    def __init__(self, listed, place, store, e):
        self.listed, self.place, self.store, self.e = listed, place, store, e

    def row(self, c):
        return self.listed[self.e * LISTED + c]

    def block(self, row, a):
        return self.store[self.place[row * WINDOW + self.row(a)]]

    def pair(self, row, a):
        return jnp.concatenate([self.block(row, a), self.block(row, a + 1)], axis=1)

    def tile(self, row0, row1, a):
        return jnp.concatenate([self.pair(row0, a), self.pair(row1, a)], axis=0)

    def times(self, left, rows, a):
        total = jnp.zeros((BS, 2 * BS), jnp.float32)
        for c in range(0, LISTED, 2):
            right = self.tile(rows[c], rows[c + 1], a)
            total += jnp.dot(left(c), right, preferred_element_type=jnp.float32)
        return total


def close_kernel(listed, place, own, inner, near, store, partial):
    for n, source in enumerate((own, inner)):
        for r in range(ROWS):
            for s in range(LISTED):
                store[n * INNER_AT + s * ROWS + r] = source[r, :, s * BS : (s + 1) * BS]
    place_share(near, store, True)
    store[ZERO] = jnp.zeros((BS, BS), jnp.bfloat16)
    whole = FAR + 2 * half()

    def one_row(e, carry):
        blocks = Blocks(listed, place, store, e)
        i = row_of(e)
        rows = []
        for c in range(LISTED):
            row = blocks.row(c)
            away = jnp.logical_and(row < ROWS, row != whole)
            rows.append(jnp.where(away, WINDOW, row))
        for a in range(0, LISTED, 2):
            partial[e, :, a * BS : (a + 2) * BS] = blocks.times(
                lambda c: own[i, :, c * BS : (c + 2) * BS], rows, a
            )
        return carry

    lax.fori_loop(0, ROWS, one_row, 0)


def chosen(blocks, low, high, index, most):
    base = blocks.e * LISTED
    for t in range(LISTED):
        index[base + t] = 0
    count = jnp.int32(0)
    for c in range(LISTED):
        row = blocks.row(c)
        index[base + count] = c
        count += jnp.logical_and(row >= low, row < high).astype(jnp.int32)
    picks = []
    for t in range(most):
        valid = t < count
        c = jnp.where(valid, index[base + t], 0)
        picks.append((c, jnp.where(valid, blocks.row(c), WINDOW)))
    return count, picks


def step(blocks, own, picks, a):
    i = row_of(blocks.e)
    left = jnp.concatenate(
        [own[i, :, pl.ds(pl.multiple_of(c * BS, BS), BS)] for c, _ in picks], axis=1
    )
    right = blocks.tile(picks[0][1], picks[1][1], a)
    return jnp.dot(left, right, preferred_element_type=jnp.float32)


def add_rows(listed, place, store, own, source, total, rows, low, high, mosts, index):
    later = []
    for e, most in zip(rows, mosts):
        blocks = Blocks(listed, place, store, e)
        count, picks = chosen(blocks, low, high, index, most)
        for a in range(0, LISTED, 2):
            cols = slice(a * BS, (a + 2) * BS)
            total[e - rows[0], :, cols] = source(e)[:, cols] + step(blocks, own, picks[:2], a)
        for t in range(2, most, 2):
            later.append((blocks, count, picks[t : t + 2], t))
    for blocks, count, picks, t in later:

        @pl.when(count > t)
        def _():
            for a in range(0, LISTED, 2):
                cols = slice(a * BS, (a + 2) * BS)
                total[blocks.e - rows[0], :, cols] += step(blocks, own, picks, a)


def finish(listed, place, store, total, rows, square, result, out, sems):
    layer = lax.axis_index("layer")
    start = pl.multiple_of(layer * 2 * BS, 2 * BS)
    copies = []
    for e in rows:
        n = e - rows[0]
        blocks = Blocks(listed, place, store, e)
        square[n] = total[n].astype(jnp.bfloat16)
        cube = blocks.times(
            lambda c: square[n, :, c * BS : (c + 2) * BS],
            [blocks.row(c) for c in range(LISTED)],
            2 * layer,
        )
        result[n] = 3.0 * square[n, :, pl.ds(start, 2 * BS)].astype(jnp.float32) - 2.0 * cube
        copies.append(pltpu.make_async_copy(result.at[n], out.at[row_of(e)], sems.at[n]))
        copies[-1].start()
    for copy in copies:
        copy.wait()


def insert(pieces, store, sems):
    copies = [
        pltpu.make_async_copy(piece, store.at[pl.ds(at, count)], sems.at[n])
        for n, (piece, at, count) in enumerate(pieces)
    ]
    for copy in copies:
        copy.start()
    for copy in copies:
        copy.wait()


def place_share(share, store, mine):
    base = NEAR_AT + SHARE * (half() if mine else 1 - half())
    for n in range(SHARE):
        store[base + n] = share[:, n * BS : (n + 1) * BS]


def swapped_kernel(
    listed, place, own, swapped, sums, _, store, rest, out, total, square, result, index, out_sems
):
    place_share(swapped, store, False)
    low = FAR + 1 - half()
    source = lambda e: sums.at[e]
    ended, left = list(range(FAR, ROWS)), list(range(FAR))
    add_rows(listed, place, store, own, source, total, ended, low, low + 2, [2] * NEAR, index)
    add_rows(listed, place, store, own, source, rest, left, low, low + 2, [2] * FAR, index)
    finish(listed, place, store, total, ended, square, result, out, out_sems)


def far_kernel(
    listed, place, own, first, last, rest, _s, _o, store, out, total, square, result, index, out_sems, sems
):
    insert([(first, FAR_AT, FIRST), (last, FAR_AT + FIRST, REST)], store, sems)
    source = lambda e: rest.at[e]
    rows = list(range(FAR))
    add_rows(listed, place, store, own, source, total, rows, 0, FAR, [6, 4, 4, 2, 2], index)
    finish(listed, place, store, total, rows, square, result, out, out_sems)


def shape(*dims, dtype=jnp.bfloat16):
    return jax.ShapeDtypeStruct(dims, dtype)


def cost(flops):
    return pl.CostEstimate(flops=flops, bytes_accessed=4_000_000, transcendentals=0)


def local(density, pattern):
    grid = lax.axis_size("grid")
    layers = lax.axis_size("layer")
    outer_pairs = [(i, (i - 1) % grid if i % 2 == 0 else (i + 1) % grid) for i in range(grid)]
    inner_pairs = [(i, i + 1 if i % 2 == 0 else i - 1) for i in range(grid)]
    swap_pairs = []
    for y in range(layers):
        for i in range(grid):
            other = (y ^ 1) if i % 2 == 0 else ((y + 1) ^ 1) - 1
            swap_pairs.append((y * grid + i, (other % layers) * grid + i))
    small = pltpu.CompilerParams(vmem_limit_bytes=8 * 2**20)
    limits = pltpu.CompilerParams(vmem_limit_bytes=24 * 2**20)

    in_hbm = pltpu.with_memory_space_constraint(density, pltpu.HBM)
    by_slot = pltpu.with_memory_space_constraint(pattern.T, pltpu.HBM)
    picked = pl.pallas_call(
        pick_kernel,
        out_shape=shape(BS, SHARE * BS),
        in_specs=[HBM],
        out_specs=VMEM,
        scratch_shapes=[pltpu.SemaphoreType.DMA((2,))],
        compiler_params=small,
        name="pick",
    )(in_hbm)
    inner_sent, picked = lax.optimization_barrier((density, picked))
    inner = lax.ppermute(inner_sent, "grid", inner_pairs)
    packing = dict(
        scratch_shapes=[
            pltpu.VMEM(by_slot.shape, jnp.int32),
            pltpu.VMEM((FAR, BS, SPAN), jnp.bfloat16),
            pltpu.VMEM((LISTED, BS), jnp.int32),
            pltpu.SMEM((LISTED, BS), jnp.int32),
            pltpu.VMEM((FAR_BLOCKS + 1, BS, BS), jnp.bfloat16),
            pltpu.SemaphoreType.DMA((3,)),
        ],
        compiler_params=small,
    )
    first_shape, rest_shape = shape(FIRST, BS, BS), shape(REST, BS, BS)
    moves_shape = jax.ShapeDtypeStruct((LISTED, BS), jnp.int32)
    first, moves, unused = pl.pallas_call(
        early_pack_kernel,
        out_shape=(first_shape, moves_shape, rest_shape),
        in_specs=[HBM, HBM],
        out_specs=(ANY, ANY, ANY),
        name="early_pack",
        **packing,
    )(by_slot, in_hbm)
    picked, first = lax.optimization_barrier((picked, first))
    near = lax.ppermute(picked, "grid", outer_pairs)
    first, moves = pl.pallas_call(
        late_pack_kernel,
        out_shape=(first_shape, moves_shape),
        in_specs=[HBM, HBM, ANY, ANY],
        out_specs=(ANY, ANY),
        input_output_aliases={2: 0, 3: 1},
        name="late_pack",
        **packing,
    )(by_slot, in_hbm, first, moves)
    first = lax.ppermute(first, "grid", outer_pairs)

    def send_rest(_):
        rest = pl.pallas_call(
            pack_rest_kernel,
            out_shape=(rest_shape, moves_shape),
            in_specs=[HBM, HBM],
            out_specs=(ANY, ANY),
            name="pack_rest",
            **packing,
        )(by_slot, in_hbm)[0]
        return lax.ppermute(rest, "grid", outer_pairs)

    last = lax.cond(moves[0, BS - 1] > 0, send_rest, lambda blocks: blocks, unused)

    listed, place = tables(pattern, moves)
    near, listed, place, last = lax.optimization_barrier((near, listed, place, last))
    store_shape = shape(STORE, BS, BS)
    out_shape = shape(ROWS, BS, 2 * BS, dtype=jnp.float32)

    def working(rows):
        return [
            pltpu.VMEM((rows, BS, SPAN), jnp.float32),
            pltpu.VMEM((rows, BS, SPAN), jnp.bfloat16),
            pltpu.VMEM((rows, BS, 2 * BS), jnp.float32),
            pltpu.SMEM((ROWS * LISTED,), jnp.int32),
            pltpu.SemaphoreType.DMA((rows,)),
        ]

    swapped = lax.ppermute(near, ("layer", "grid"), swap_pairs)
    store, sums = pl.pallas_call(
        close_kernel,
        out_shape=(store_shape, shape(ROWS, BS, SPAN, dtype=jnp.float32)),
        in_specs=[SMEM, SMEM, VMEM, VMEM, VMEM],
        out_specs=(VMEM, VMEM),
        compiler_params=limits,
        cost_estimate=cost(4_000_000_000),
        name="close",
    )(listed, place, density, inner, near)
    store, rest, out = pl.pallas_call(
        swapped_kernel,
        out_shape=(store_shape, shape(FAR, BS, SPAN, dtype=jnp.float32), out_shape),
        in_specs=[SMEM, SMEM] + [VMEM] * 4,
        out_specs=(VMEM, VMEM, ANY),
        scratch_shapes=working(NEAR),
        input_output_aliases={5: 0},
        compiler_params=limits,
        cost_estimate=cost(2_000_000_000),
        name="swapped",
    )(listed, place, density, swapped, sums, store)
    return pl.pallas_call(
        far_kernel,
        out_shape=(store_shape, out_shape),
        in_specs=[SMEM, SMEM] + [VMEM] * 5 + [ANY],
        out_specs=(VMEM, ANY),
        scratch_shapes=working(FAR) + [pltpu.SemaphoreType.DMA((2,))],
        input_output_aliases={6: 0, 7: 1},
        compiler_params=limits,
        cost_estimate=cost(2_000_000_000),
        name="far",
    )(listed, place, density, first, last, rest, store, out)[1]


def solution(mesh):
    placed = (P("grid", None, None), P())
    return jax.shard_map(
        local, mesh=mesh, in_specs=placed, out_specs=P("grid", None, "layer"), check_vma=False
    )
```

```python
import jax
import jax.numpy as jnp
import numpy as np
from jax import lax
from jax.experimental import pallas as pl
from jax.experimental.pallas import tpu as pltpu
from jax.sharding import PartitionSpec as P

ROWS = 8
LISTED = 8
BS = 128
SPAN = LISTED * BS
WINDOW = 3 * ROWS
FAR = 5
NEAR = ROWS - FAR
SHARE = NEAR * LISTED // 2
FAR_BLOCKS = FAR * LISTED
FIRST = 28
REST = FAR_BLOCKS - FIRST
EARLY_EVERY = 16
INNER_AT = ROWS * LISTED
NEAR_AT = 2 * ROWS * LISTED
FAR_AT = NEAR_AT + 2 * SHARE
ZERO = FAR_AT + FAR_BLOCKS
STORE = ZERO + 1

ANY = pl.BlockSpec(memory_space=pl.ANY)
HBM = pl.BlockSpec(memory_space=pltpu.HBM)
SMEM = pl.BlockSpec(memory_space=pltpu.SMEM)
VMEM = pl.BlockSpec(memory_space=pltpu.VMEM)


def places(odd):
    middle = LISTED // 2
    rows = [
        [NEAR_AT + s for s in range(LISTED)],
        [NEAR_AT + LISTED + s + (SHARE - middle if s >= middle else 0) for s in range(LISTED)],
        [NEAR_AT + SHARE + s for s in range(LISTED)],
    ]
    for base in (0, INNER_AT):
        for e in range(ROWS):
            i = ROWS - 1 - e if odd else e
            rows.append([base + s * ROWS + i for s in range(LISTED)])
    rows.append([ZERO] * LISTED)
    return np.array(rows, np.int32)


def tables(pattern, moves):
    blocks = pattern.shape[0]
    g = lax.axis_index("grid")
    odd = g % 2 == 1
    first = g * ROWS - ROWS
    ring = jnp.concatenate([pattern[-ROWS:], pattern, pattern[:ROWS]], axis=0)
    columns = lax.dynamic_slice_in_dim(ring, g * ROWS, WINDOW, 0) - first
    columns = jnp.where(columns >= blocks, columns - blocks, columns)
    columns = jnp.where(columns < 0, columns + blocks, columns)
    columns = jnp.where(odd, WINDOW - 1 - columns[::-1], columns)
    listed = columns[ROWS : 2 * ROWS]
    columns = jnp.concatenate([columns, jnp.full((1, LISTED), -1, jnp.int32)], axis=0)
    at = jnp.where(odd, places(True), places(False))
    far = jnp.where(odd, moves[:, WINDOW - FAR : WINDOW][:, ::-1], moves[:, :FAR]).T
    far = jnp.where(far == FAR_BLOCKS, ZERO, FAR_AT + far)
    at = jnp.concatenate([far, at], axis=0)
    xs = lax.broadcasted_iota(jnp.int32, (WINDOW + 1, WINDOW), 1)
    place = jnp.full((WINDOW + 1, WINDOW), ZERO, jnp.int32)
    for s in range(LISTED):
        place = jnp.where(columns[:, s : s + 1] == xs, at[:, s : s + 1], place)
    return listed.reshape(-1), place.reshape(-1)


def ones(bits):
    bits = (bits & 0x55555555) + ((bits >> 1) & 0x55555555)
    bits = (bits & 0x33333333) + ((bits >> 2) & 0x33333333)
    bits = (bits & 0x0F0F0F0F) + ((bits >> 4) & 0x0F0F0F0F)
    bits = bits + (bits >> 8)
    return (bits + (bits >> 16)) & 0xFF


def positions(pattern):
    blocks = pattern.shape[1]
    row = lax.broadcasted_iota(jnp.int32, pattern.shape, 1)
    slot = lax.broadcasted_iota(jnp.int32, pattern.shape, 0)
    offset = pattern - row + ROWS
    offset = jnp.where(offset < 0, offset + blocks, offset)
    offset = jnp.where(offset >= blocks, offset - blocks, offset)
    bits = jnp.sum(jnp.left_shift(1, offset), axis=0, keepdims=True)
    bits = jnp.broadcast_to(bits, pattern.shape)
    k = row & (ROWS - 1)
    forward = (row & ROWS) != 0
    uses = jnp.zeros(pattern.shape, jnp.int32)
    for d in range(1, ROWS + 1):
        after = pltpu.roll(bits, blocks - d, 1)
        before = pltpu.roll(bits, d, 1)
        hit_after = jnp.logical_and(k + d >= ROWS, ((after >> (ROWS - d)) & 1) == 1)
        hit_before = jnp.logical_and(k - d < 0, ((before >> (ROWS + d)) & 1) == 1)
        uses = uses | jnp.where(
            forward, jnp.where(hit_after, after << d, 0), jnp.where(hit_before, before >> d, 0)
        )
    far = jnp.where(forward, k, ROWS - 1 - k) < FAR
    mask = jnp.where(far, bits & uses, 0)
    sent = (mask >> offset) & 1
    up_to = sent
    for d in (1, 2, 4):
        up_to = up_to + jnp.where(slot >= d, pltpu.roll(up_to, d, 0), 0)
    count = ones(mask)
    ahead, behind = count, count
    for d in (1, 2, 4):
        ahead = ahead + jnp.where(k >= d, pltpu.roll(ahead, d, 1), 0)
        behind = behind + jnp.where(k < ROWS - d, pltpu.roll(behind, blocks - d, 1), 0)
    position = jnp.where(forward, ahead, behind) - count + up_to - sent
    most = jnp.max(ahead.astype(jnp.float32))
    return jnp.where(sent == 1, position, FAR_BLOCKS), most


def parity():
    return lax.rem(lax.axis_index("grid"), 2)


def half():
    return lax.rem(lax.axis_index("layer"), 2)


def row_of(e):
    return jnp.where(parity() == 0, e, ROWS - 1 - e)


def sent_row(w):
    return jnp.where(parity() == 1, w, ROWS - 1 - w)


def pick_kernel(source, out, sems):
    whole = sent_row(FAR + 2 * half())
    start = pl.multiple_of(half() * (SPAN // 2), SPAN // 2)
    copies = [
        pltpu.make_async_copy(source.at[whole], out.at[:, pl.ds(0, SPAN)], sems.at[0]),
        pltpu.make_async_copy(
            source.at[sent_row(FAR + 1), :, pl.ds(start, SPAN // 2)], out.at[:, pl.ds(SPAN, SPAN // 2)], sems.at[1]
        ),
    ]
    for copy in copies:
        copy.start()
    for copy in copies:
        copy.wait()


def waits_long():
    return lax.rem(lax.axis_index("grid"), EARLY_EVERY) == 0


def pack(first, count, pattern, source, out, moves, listed, own, window, places, packed, sems):
    fetch = pltpu.make_async_copy(pattern, listed, sems.at[0])
    fetch.start()
    start = jnp.where(parity() == 1, 0, ROWS - FAR)
    rows = pltpu.make_async_copy(source.at[pl.ds(start, FAR)], own, sems.at[1])
    rows.start()
    fetch.wait()
    position, most = positions(listed[...])
    blocks, grid = pattern.shape[1], lax.axis_size("grid")
    shift = blocks - ROWS * lax.rem(lax.axis_index("grid") + grid - 1, grid)
    position = pltpu.roll(position, lax.rem(shift, blocks), 1)[:, :BS]
    lane = lax.broadcasted_iota(jnp.int32, position.shape, 1)
    window[...] = jnp.where(lane == BS - 1, (most > FIRST).astype(jnp.int32), position)
    scalars = pltpu.make_async_copy(window, places, sems.at[0])
    scalars.start()
    table = pltpu.make_async_copy(window, moves, sems.at[2])
    table.start()
    scalars.wait()
    rows.wait()
    for k in range(FAR):
        held = jnp.where(parity() == 1, k, FAR - 1 - k)
        for s in range(LISTED):
            packed[places[s, ROWS + sent_row(k)]] = own[held, :, s * BS : (s + 1) * BS]
    copy = pltpu.make_async_copy(packed.at[pl.ds(first, count)], out, sems.at[0])
    copy.start()
    copy.wait()
    table.wait()


def early_pack_kernel(pattern, source, first, moves, unused, *scratch):
    @pl.when(waits_long())
    def _():
        pack(0, FIRST, pattern, source, first, moves, *scratch)


def late_pack_kernel(pattern, source, _f, _m, first, moves, *scratch):
    @pl.when(jnp.logical_not(waits_long()))
    def _():
        pack(0, FIRST, pattern, source, first, moves, *scratch)


def pack_rest_kernel(*refs):
    pack(FIRST, REST, *refs)


class Blocks:
    def __init__(self, listed, place, store, e):
        self.listed, self.place, self.store, self.e = listed, place, store, e

    def row(self, c):
        return self.listed[self.e * LISTED + c]

    def block(self, row, a):
        return self.store[self.place[row * WINDOW + self.row(a)]]

    def pair(self, row, a):
        return jnp.concatenate([self.block(row, a), self.block(row, a + 1)], axis=1)

    def tile(self, row0, row1, a):
        return jnp.concatenate([self.pair(row0, a), self.pair(row1, a)], axis=0)

    def times(self, left, rows, a):
        total = jnp.zeros((BS, 2 * BS), jnp.float32)
        for c in range(0, LISTED, 2):
            right = self.tile(rows[c], rows[c + 1], a)
            total += jnp.dot(left(c), right, preferred_element_type=jnp.float32)
        return total


def close_kernel(listed, place, own_hbm, inner, near, last, store, partial, own, other, sems):
    count = ROWS // 4
    fetches = [
        pltpu.make_async_copy(source.at[pl.ds(r, count)], held.at[pl.ds(r, count)], sems.at[n, r // count])
        for n, (source, held) in enumerate(((own_hbm, own), (inner, other)))
        for r in range(0, ROWS, count)
    ]
    fill = pltpu.make_async_copy(last, store.at[pl.ds(FAR_AT + FIRST, REST)], sems.at[2, 0])
    for copy in fetches:
        copy.start()
    fill.start()
    for n, held in enumerate((own, other)):
        for r in range(ROWS):
            if r % count == 0:
                fetches[n * (ROWS // count) + r // count].wait()
            for s in range(LISTED):
                store[n * INNER_AT + s * ROWS + r] = held[r, :, s * BS : (s + 1) * BS]
    place_share(near, store, True)
    store[ZERO] = jnp.zeros((BS, BS), jnp.bfloat16)
    whole = FAR + 2 * half()

    def one_row(e, carry):
        blocks = Blocks(listed, place, store, e)
        i = row_of(e)
        rows = []
        for c in range(LISTED):
            row = blocks.row(c)
            away = jnp.logical_and(row < ROWS, row != whole)
            rows.append(jnp.where(away, WINDOW, row))
        for a in range(0, LISTED, 2):
            partial[e, :, a * BS : (a + 2) * BS] = blocks.times(
                lambda c: own[i, :, c * BS : (c + 2) * BS], rows, a
            )
        return carry

    lax.fori_loop(0, ROWS, one_row, 0, unroll=2)
    fill.wait()


def chosen(blocks, low, high, index, most):
    base = blocks.e * LISTED
    for t in range(LISTED):
        index[base + t] = 0
    count = jnp.int32(0)
    for c in range(LISTED):
        row = blocks.row(c)
        index[base + count] = c
        count += jnp.logical_and(row >= low, row < high).astype(jnp.int32)
    picks = []
    for t in range(most):
        valid = t < count
        c = jnp.where(valid, index[base + t], 0)
        picks.append((c, jnp.where(valid, blocks.row(c), WINDOW)))
    return count, picks


def step(blocks, own, picks, a):
    i = row_of(blocks.e)
    left = jnp.concatenate(
        [own[i, :, pl.ds(pl.multiple_of(c * BS, BS), BS)] for c, _ in picks], axis=1
    )
    right = blocks.tile(picks[0][1], picks[1][1], a)
    return jnp.dot(left, right, preferred_element_type=jnp.float32)


def add_rows(listed, place, store, own, source, total, rows, low, high, mosts, index):
    later = []
    for e, most in zip(rows, mosts):
        blocks = Blocks(listed, place, store, e)
        count, picks = chosen(blocks, low, high, index, most)
        for a in range(0, LISTED, 2):
            cols = slice(a * BS, (a + 2) * BS)
            total[e - rows[0], :, cols] = source(e)[:, cols] + step(blocks, own, picks[:2], a)
        for t in range(2, most, 2):
            later.append((blocks, count, picks[t : t + 2], t))
    for blocks, count, picks, t in later:

        @pl.when(count > t)
        def _():
            for a in range(0, LISTED, 2):
                cols = slice(a * BS, (a + 2) * BS)
                total[blocks.e - rows[0], :, cols] += step(blocks, own, picks, a)


def finish(listed, place, store, total, rows, square, result, out, sems):
    layer = lax.axis_index("layer")
    start = pl.multiple_of(layer * 2 * BS, 2 * BS)
    copies = []
    for e in rows:
        n = e - rows[0]
        blocks = Blocks(listed, place, store, e)
        square[n] = total[n].astype(jnp.bfloat16)
        cube = blocks.times(
            lambda c: square[n, :, c * BS : (c + 2) * BS],
            [blocks.row(c) for c in range(LISTED)],
            2 * layer,
        )
        result[n] = 3.0 * square[n, :, pl.ds(start, 2 * BS)].astype(jnp.float32) - 2.0 * cube
        copies.append(pltpu.make_async_copy(result.at[n], out.at[row_of(e)], sems.at[n]))
        copies[-1].start()
    for copy in copies:
        copy.wait()


def insert(pieces, store, sems):
    copies = [
        pltpu.make_async_copy(piece, store.at[pl.ds(at, count)], sems.at[n])
        for n, (piece, at, count) in enumerate(pieces)
    ]
    for copy in copies:
        copy.start()
    for copy in copies:
        copy.wait()


def place_share(share, store, mine):
    base = NEAR_AT + SHARE * (half() if mine else 1 - half())
    for n in range(SHARE):
        store[base + n] = share[:, n * BS : (n + 1) * BS]


def swapped_kernel(
    listed, place, own, swapped, sums, _, store, rest, out, total, square, result, index, out_sems
):
    place_share(swapped, store, False)
    low = FAR + 1 - half()
    source = lambda e: sums.at[e]
    ended, left = list(range(FAR, ROWS)), list(range(FAR))
    add_rows(listed, place, store, own, source, total, ended, low, low + 2, [2] * NEAR, index)
    add_rows(listed, place, store, own, source, rest, left, low, low + 2, [2] * FAR, index)
    finish(listed, place, store, total, ended, square, result, out, out_sems)


def far_kernel(
    listed, place, own, first, rest, _s, _o, store, out, total, square, result, index, out_sems, sems
):
    insert([(first, FAR_AT, FIRST)], store, sems)
    source = lambda e: rest.at[e]
    rows = list(range(FAR))
    add_rows(listed, place, store, own, source, total, rows, 0, FAR, [6, 4, 4, 2, 2], index)
    finish(listed, place, store, total, rows, square, result, out, out_sems)


def shape(*dims, dtype=jnp.bfloat16):
    return jax.ShapeDtypeStruct(dims, dtype)


def cost(flops):
    return pl.CostEstimate(flops=flops, bytes_accessed=4_000_000, transcendentals=0)


def local(density, pattern):
    grid = lax.axis_size("grid")
    layers = lax.axis_size("layer")
    outer_pairs = [(i, (i - 1) % grid if i % 2 == 0 else (i + 1) % grid) for i in range(grid)]
    inner_pairs = [(i, i + 1 if i % 2 == 0 else i - 1) for i in range(grid)]
    swap_pairs = []
    for y in range(layers):
        for i in range(grid):
            other = (y ^ 1) if i % 2 == 0 else ((y + 1) ^ 1) - 1
            swap_pairs.append((y * grid + i, (other % layers) * grid + i))
    small = pltpu.CompilerParams(vmem_limit_bytes=8 * 2**20)
    limits = pltpu.CompilerParams(vmem_limit_bytes=24 * 2**20)

    in_hbm = pltpu.with_memory_space_constraint(density, pltpu.HBM)
    by_slot = pltpu.with_memory_space_constraint(pattern.T, pltpu.HBM)
    picked = pl.pallas_call(
        pick_kernel,
        out_shape=shape(BS, SHARE * BS),
        in_specs=[HBM],
        out_specs=VMEM,
        scratch_shapes=[pltpu.SemaphoreType.DMA((2,))],
        compiler_params=small,
        name="pick",
    )(in_hbm)
    inner_sent, picked = lax.optimization_barrier((density, picked))
    inner = lax.ppermute(inner_sent, "grid", inner_pairs)
    packing = dict(
        scratch_shapes=[
            pltpu.VMEM(by_slot.shape, jnp.int32),
            pltpu.VMEM((FAR, BS, SPAN), jnp.bfloat16),
            pltpu.VMEM((LISTED, BS), jnp.int32),
            pltpu.SMEM((LISTED, BS), jnp.int32),
            pltpu.VMEM((FAR_BLOCKS + 1, BS, BS), jnp.bfloat16),
            pltpu.SemaphoreType.DMA((3,)),
        ],
        compiler_params=small,
    )
    first_shape, rest_shape = shape(FIRST, BS, BS), shape(REST, BS, BS)
    moves_shape = jax.ShapeDtypeStruct((LISTED, BS), jnp.int32)
    first, moves, unused = pl.pallas_call(
        early_pack_kernel,
        out_shape=(first_shape, moves_shape, rest_shape),
        in_specs=[HBM, HBM],
        out_specs=(ANY, ANY, ANY),
        name="early_pack",
        **packing,
    )(by_slot, in_hbm)
    picked, first = lax.optimization_barrier((picked, first))
    near = lax.ppermute(picked, "grid", outer_pairs)
    first, moves = pl.pallas_call(
        late_pack_kernel,
        out_shape=(first_shape, moves_shape),
        in_specs=[HBM, HBM, ANY, ANY],
        out_specs=(ANY, ANY),
        input_output_aliases={2: 0, 3: 1},
        name="late_pack",
        **packing,
    )(by_slot, in_hbm, first, moves)
    first = lax.ppermute(first, "grid", outer_pairs)

    def send_rest(_):
        rest = pl.pallas_call(
            pack_rest_kernel,
            out_shape=(rest_shape, moves_shape),
            in_specs=[HBM, HBM],
            out_specs=(ANY, ANY),
            name="pack_rest",
            **packing,
        )(by_slot, in_hbm)[0]
        return lax.ppermute(rest, "grid", outer_pairs)

    last = lax.cond(moves[0, BS - 1] > 0, send_rest, lambda blocks: blocks, unused)

    listed, place = tables(pattern, moves)
    near, listed, place, last = lax.optimization_barrier((near, listed, place, last))
    store_shape = shape(STORE, BS, BS)
    out_shape = shape(ROWS, BS, 2 * BS, dtype=jnp.float32)

    def working(rows):
        return [
            pltpu.VMEM((rows, BS, SPAN), jnp.float32),
            pltpu.VMEM((rows, BS, SPAN), jnp.bfloat16),
            pltpu.VMEM((rows, BS, 2 * BS), jnp.float32),
            pltpu.SMEM((ROWS * LISTED,), jnp.int32),
            pltpu.SemaphoreType.DMA((rows,)),
        ]

    swapped = lax.ppermute(near, ("layer", "grid"), swap_pairs)
    store, sums = pl.pallas_call(
        close_kernel,
        out_shape=(store_shape, shape(ROWS, BS, SPAN, dtype=jnp.float32)),
        in_specs=[SMEM, SMEM, HBM, ANY, VMEM, ANY],
        out_specs=(VMEM, VMEM),
        scratch_shapes=[
            pltpu.VMEM(density.shape, density.dtype),
            pltpu.VMEM(density.shape, density.dtype),
            pltpu.SemaphoreType.DMA((3, 4)),
        ],
        compiler_params=limits,
        cost_estimate=cost(4_000_000_000),
        name="close",
    )(listed, place, in_hbm, inner, near, last)
    store, rest, out = pl.pallas_call(
        swapped_kernel,
        out_shape=(store_shape, shape(FAR, BS, SPAN, dtype=jnp.float32), out_shape),
        in_specs=[SMEM, SMEM] + [VMEM] * 4,
        out_specs=(VMEM, VMEM, ANY),
        scratch_shapes=working(NEAR),
        input_output_aliases={5: 0},
        compiler_params=limits,
        cost_estimate=cost(2_000_000_000),
        name="swapped",
    )(listed, place, density, swapped, sums, store)
    return pl.pallas_call(
        far_kernel,
        out_shape=(store_shape, out_shape),
        in_specs=[SMEM, SMEM] + [VMEM] * 4 + [ANY],
        out_specs=(VMEM, ANY),
        scratch_shapes=working(FAR) + [pltpu.SemaphoreType.DMA((1,))],
        input_output_aliases={5: 0, 6: 1},
        compiler_params=limits,
        cost_estimate=cost(2_000_000_000),
        name="far",
    )(listed, place, density, first, rest, store, out)[1]


def solution(mesh):
    placed = (P("grid", None, None), P())
    return jax.shard_map(
        local, mesh=mesh, in_specs=placed, out_specs=P("grid", None, "layer"), check_vma=False
    )
```

```python
import jax
import jax.numpy as jnp
import numpy as np
from jax import lax
from jax.experimental import pallas as pl
from jax.experimental.pallas import tpu as pltpu
from jax.sharding import PartitionSpec as P

ROWS = 8
LISTED = 8
BS = 128
SPAN = LISTED * BS
WINDOW = 3 * ROWS
FAR = 5
NEAR = ROWS - FAR
SHARE = NEAR * LISTED // 2
FAR_BLOCKS = FAR * LISTED
FIRST = 27
REST = FAR_BLOCKS - FIRST
EARLY_EVERY = 16
INNER_AT = ROWS * LISTED
NEAR_AT = 2 * ROWS * LISTED
FAR_AT = NEAR_AT + 2 * SHARE
ZERO = FAR_AT + FAR_BLOCKS
STORE = ZERO + 1

ANY = pl.BlockSpec(memory_space=pl.ANY)
HBM = pl.BlockSpec(memory_space=pltpu.HBM)
SMEM = pl.BlockSpec(memory_space=pltpu.SMEM)
VMEM = pl.BlockSpec(memory_space=pltpu.VMEM)


def places(odd):
    middle = LISTED // 2
    rows = [
        [NEAR_AT + s for s in range(LISTED)],
        [NEAR_AT + LISTED + s + (SHARE - middle if s >= middle else 0) for s in range(LISTED)],
        [NEAR_AT + SHARE + s for s in range(LISTED)],
    ]
    for base in (0, INNER_AT):
        for e in range(ROWS):
            i = ROWS - 1 - e if odd else e
            rows.append([base + s * ROWS + i for s in range(LISTED)])
    rows.append([ZERO] * LISTED)
    return np.array(rows, np.int32)


def tables(pattern, moves):
    blocks = pattern.shape[0]
    g = lax.axis_index("grid")
    odd = g % 2 == 1
    first = g * ROWS - ROWS
    ring = jnp.concatenate([pattern[-ROWS:], pattern, pattern[:ROWS]], axis=0)
    columns = lax.dynamic_slice_in_dim(ring, g * ROWS, WINDOW, 0) - first
    columns = jnp.where(columns >= blocks, columns - blocks, columns)
    columns = jnp.where(columns < 0, columns + blocks, columns)
    columns = jnp.where(odd, WINDOW - 1 - columns[::-1], columns)
    listed = columns[ROWS : 2 * ROWS]
    columns = jnp.concatenate([columns, jnp.full((1, LISTED), -1, jnp.int32)], axis=0)
    at = jnp.where(odd, places(True), places(False))
    far = jnp.where(odd, moves[:, WINDOW - FAR : WINDOW][:, ::-1], moves[:, :FAR]).T
    far = jnp.where(far == FAR_BLOCKS, ZERO, FAR_AT + far)
    at = jnp.concatenate([far, at], axis=0)
    xs = lax.broadcasted_iota(jnp.int32, (WINDOW + 1, WINDOW), 1)
    place = jnp.full((WINDOW + 1, WINDOW), ZERO, jnp.int32)
    for s in range(LISTED):
        place = jnp.where(columns[:, s : s + 1] == xs, at[:, s : s + 1], place)
    return listed.reshape(-1), place.reshape(-1)


def ones(bits):
    bits = (bits & 0x55555555) + ((bits >> 1) & 0x55555555)
    bits = (bits & 0x33333333) + ((bits >> 2) & 0x33333333)
    bits = (bits & 0x0F0F0F0F) + ((bits >> 4) & 0x0F0F0F0F)
    bits = bits + (bits >> 8)
    return (bits + (bits >> 16)) & 0xFF


def positions(pattern):
    blocks = pattern.shape[1]
    row = lax.broadcasted_iota(jnp.int32, pattern.shape, 1)
    slot = lax.broadcasted_iota(jnp.int32, pattern.shape, 0)
    offset = pattern - row + ROWS
    offset = jnp.where(offset < 0, offset + blocks, offset)
    offset = jnp.where(offset >= blocks, offset - blocks, offset)
    bits = jnp.sum(jnp.left_shift(1, offset), axis=0, keepdims=True)
    bits = jnp.broadcast_to(bits, pattern.shape)
    k = row & (ROWS - 1)
    forward = (row & ROWS) != 0
    uses = jnp.zeros(pattern.shape, jnp.int32)
    for d in range(1, ROWS + 1):
        after = pltpu.roll(bits, blocks - d, 1)
        before = pltpu.roll(bits, d, 1)
        hit_after = jnp.logical_and(k + d >= ROWS, ((after >> (ROWS - d)) & 1) == 1)
        hit_before = jnp.logical_and(k - d < 0, ((before >> (ROWS + d)) & 1) == 1)
        uses = uses | jnp.where(
            forward, jnp.where(hit_after, after << d, 0), jnp.where(hit_before, before >> d, 0)
        )
    far = jnp.where(forward, k, ROWS - 1 - k) < FAR
    mask = jnp.where(far, bits & uses, 0)
    sent = (mask >> offset) & 1
    up_to = sent
    for d in (1, 2, 4):
        up_to = up_to + jnp.where(slot >= d, pltpu.roll(up_to, d, 0), 0)
    count = ones(mask)
    ahead, behind = count, count
    for d in (1, 2, 4):
        ahead = ahead + jnp.where(k >= d, pltpu.roll(ahead, d, 1), 0)
        behind = behind + jnp.where(k < ROWS - d, pltpu.roll(behind, blocks - d, 1), 0)
    position = jnp.where(forward, ahead, behind) - count + up_to - sent
    most = jnp.max(ahead.astype(jnp.float32))
    return jnp.where(sent == 1, position, FAR_BLOCKS), most


def parity():
    return lax.rem(lax.axis_index("grid"), 2)


def half():
    return lax.rem(lax.axis_index("layer"), 2)


def row_of(e):
    return jnp.where(parity() == 0, e, ROWS - 1 - e)


def sent_row(w):
    return jnp.where(parity() == 1, w, ROWS - 1 - w)


def pick_kernel(source, out, sems):
    whole = sent_row(FAR + 2 * half())
    start = pl.multiple_of(half() * (SPAN // 2), SPAN // 2)
    copies = [
        pltpu.make_async_copy(source.at[whole], out.at[:, pl.ds(0, SPAN)], sems.at[0]),
        pltpu.make_async_copy(
            source.at[sent_row(FAR + 1), :, pl.ds(start, SPAN // 2)], out.at[:, pl.ds(SPAN, SPAN // 2)], sems.at[1]
        ),
    ]
    for copy in copies:
        copy.start()
    for copy in copies:
        copy.wait()


def waits_long():
    return lax.rem(lax.axis_index("grid"), EARLY_EVERY) == 0


def pack(first, count, pattern, source, out, moves, listed, own, window, places, packed, sems):
    fetch = pltpu.make_async_copy(pattern, listed, sems.at[0])
    fetch.start()
    start = jnp.where(parity() == 1, 0, ROWS - FAR)
    rows = pltpu.make_async_copy(source.at[pl.ds(start, FAR)], own, sems.at[1])
    rows.start()
    fetch.wait()
    position, most = positions(listed[...])
    blocks, grid = pattern.shape[1], lax.axis_size("grid")
    shift = blocks - ROWS * lax.rem(lax.axis_index("grid") + grid - 1, grid)
    position = pltpu.roll(position, lax.rem(shift, blocks), 1)[:, :BS]
    lane = lax.broadcasted_iota(jnp.int32, position.shape, 1)
    window[...] = jnp.where(lane == BS - 1, (most > FIRST).astype(jnp.int32), position)
    scalars = pltpu.make_async_copy(window, places, sems.at[0])
    scalars.start()
    table = pltpu.make_async_copy(window, moves, sems.at[2])
    table.start()
    scalars.wait()
    rows.wait()
    for k in range(FAR):
        held = jnp.where(parity() == 1, k, FAR - 1 - k)
        for s in range(LISTED):
            packed[places[s, ROWS + sent_row(k)]] = own[held, :, s * BS : (s + 1) * BS]
    copy = pltpu.make_async_copy(packed.at[pl.ds(first, count)], out, sems.at[0])
    copy.start()
    copy.wait()
    table.wait()


def early_pack_kernel(pattern, source, first, moves, unused, *scratch):
    @pl.when(waits_long())
    def _():
        pack(0, FIRST, pattern, source, first, moves, *scratch)


def late_pack_kernel(pattern, source, _f, _m, first, moves, *scratch):
    @pl.when(jnp.logical_not(waits_long()))
    def _():
        pack(0, FIRST, pattern, source, first, moves, *scratch)


def pack_rest_kernel(*refs):
    pack(FIRST, REST, *refs)


class Blocks:
    def __init__(self, listed, place, store, e):
        self.listed, self.place, self.store, self.e = listed, place, store, e

    def row(self, c):
        return self.listed[self.e * LISTED + c]

    def block(self, row, a):
        return self.store[self.place[row * WINDOW + self.row(a)]]

    def pair(self, row, a):
        return jnp.concatenate([self.block(row, a), self.block(row, a + 1)], axis=1)

    def tile(self, row0, row1, a):
        return jnp.concatenate([self.pair(row0, a), self.pair(row1, a)], axis=0)

    def times(self, left, rows, a):
        total = jnp.zeros((BS, 2 * BS), jnp.float32)
        for c in range(0, LISTED, 2):
            right = self.tile(rows[c], rows[c + 1], a)
            total += jnp.dot(left(c), right, preferred_element_type=jnp.float32)
        return total


def close_kernel(listed, place, own_hbm, inner, near, last, store, partial, own, other, sems):
    count = ROWS // 4
    fetches = [
        pltpu.make_async_copy(source.at[pl.ds(r, count)], held.at[pl.ds(r, count)], sems.at[n, r // count])
        for n, (source, held) in enumerate(((own_hbm, own), (inner, other)))
        for r in range(0, ROWS, count)
    ]
    fill = pltpu.make_async_copy(last, store.at[pl.ds(FAR_AT + FIRST, REST)], sems.at[2, 0])
    for copy in fetches:
        copy.start()
    fill.start()
    for n, held in enumerate((own, other)):
        for r in range(ROWS):
            if r % count == 0:
                fetches[n * (ROWS // count) + r // count].wait()
            for s in range(LISTED):
                store[n * INNER_AT + s * ROWS + r] = held[r, :, s * BS : (s + 1) * BS]
    place_share(near, store, True)
    store[ZERO] = jnp.zeros((BS, BS), jnp.bfloat16)
    whole = FAR + 2 * half()

    def one_row(e, carry):
        blocks = Blocks(listed, place, store, e)
        i = row_of(e)
        rows = []
        for c in range(LISTED):
            row = blocks.row(c)
            away = jnp.logical_and(row < ROWS, row != whole)
            rows.append(jnp.where(away, WINDOW, row))
        for a in range(0, LISTED, 2):
            partial[e, :, a * BS : (a + 2) * BS] = blocks.times(
                lambda c: own[i, :, c * BS : (c + 2) * BS], rows, a
            )
        return carry

    lax.fori_loop(0, ROWS, one_row, 0, unroll=2)
    fill.wait()


def chosen(blocks, low, high, index, most):
    base = blocks.e * LISTED
    for t in range(LISTED):
        index[base + t] = 0
    count = jnp.int32(0)
    for c in range(LISTED):
        row = blocks.row(c)
        index[base + count] = c
        count += jnp.logical_and(row >= low, row < high).astype(jnp.int32)
    picks = []
    for t in range(most):
        valid = t < count
        c = jnp.where(valid, index[base + t], 0)
        picks.append((c, jnp.where(valid, blocks.row(c), WINDOW)))
    return count, picks


def step(blocks, own, picks, a):
    i = row_of(blocks.e)
    left = jnp.concatenate(
        [own[i, :, pl.ds(pl.multiple_of(c * BS, BS), BS)] for c, _ in picks], axis=1
    )
    right = blocks.tile(picks[0][1], picks[1][1], a)
    return jnp.dot(left, right, preferred_element_type=jnp.float32)


def add_rows(listed, place, store, own, source, total, rows, low, high, mosts, index):
    later = []
    for e, most in zip(rows, mosts):
        blocks = Blocks(listed, place, store, e)
        count, picks = chosen(blocks, low, high, index, most)
        for a in range(0, LISTED, 2):
            cols = slice(a * BS, (a + 2) * BS)
            total[e - rows[0], :, cols] = source(e)[:, cols] + step(blocks, own, picks[:2], a)
        for t in range(2, most, 2):
            later.append((blocks, count, picks[t : t + 2], t))
    for blocks, count, picks, t in later:

        @pl.when(count > t)
        def _():
            for a in range(0, LISTED, 2):
                cols = slice(a * BS, (a + 2) * BS)
                total[blocks.e - rows[0], :, cols] += step(blocks, own, picks, a)


def finish(listed, place, store, total, rows, square, result, out, sems):
    layer = lax.axis_index("layer")
    start = pl.multiple_of(layer * 2 * BS, 2 * BS)
    copies = []
    for e in rows:
        n = e - rows[0]
        blocks = Blocks(listed, place, store, e)
        square[n] = total[n].astype(jnp.bfloat16)
        cube = blocks.times(
            lambda c: square[n, :, c * BS : (c + 2) * BS],
            [blocks.row(c) for c in range(LISTED)],
            2 * layer,
        )
        result[n] = 3.0 * square[n, :, pl.ds(start, 2 * BS)].astype(jnp.float32) - 2.0 * cube
        copies.append(pltpu.make_async_copy(result.at[n], out.at[row_of(e)], sems.at[n]))
        copies[-1].start()
    for copy in copies:
        copy.wait()


def insert(pieces, store, sems):
    copies = [
        pltpu.make_async_copy(piece, store.at[pl.ds(at, count)], sems.at[n])
        for n, (piece, at, count) in enumerate(pieces)
    ]
    for copy in copies:
        copy.start()
    for copy in copies:
        copy.wait()


def place_share(share, store, mine):
    base = NEAR_AT + SHARE * (half() if mine else 1 - half())
    for n in range(SHARE):
        store[base + n] = share[:, n * BS : (n + 1) * BS]


def swapped_kernel(
    listed, place, own, swapped, sums, _, store, rest, out, total, square, result, index, out_sems
):
    place_share(swapped, store, False)
    low = FAR + 1 - half()
    source = lambda e: sums.at[e]
    ended, left = list(range(FAR, ROWS)), list(range(FAR))
    add_rows(listed, place, store, own, source, total, ended, low, low + 2, [2] * NEAR, index)
    add_rows(listed, place, store, own, source, rest, left, low, low + 2, [2] * FAR, index)
    finish(listed, place, store, total, ended, square, result, out, out_sems)


def far_kernel(
    listed, place, own, first, rest, _s, _o, store, out, total, square, result, index, out_sems, sems
):
    insert([(first, FAR_AT, FIRST)], store, sems)
    source = lambda e: rest.at[e]
    rows = list(range(FAR))
    add_rows(listed, place, store, own, source, total, rows, 0, FAR, [6, 4, 4, 2, 2], index)
    finish(listed, place, store, total, rows, square, result, out, out_sems)


def shape(*dims, dtype=jnp.bfloat16):
    return jax.ShapeDtypeStruct(dims, dtype)


def cost(flops):
    return pl.CostEstimate(flops=flops, bytes_accessed=4_000_000, transcendentals=0)


def local(density, pattern):
    grid = lax.axis_size("grid")
    layers = lax.axis_size("layer")
    outer_pairs = [(i, (i - 1) % grid if i % 2 == 0 else (i + 1) % grid) for i in range(grid)]
    inner_pairs = [(i, i + 1 if i % 2 == 0 else i - 1) for i in range(grid)]
    swap_pairs = []
    for y in range(layers):
        for i in range(grid):
            other = (y ^ 1) if i % 2 == 0 else ((y + 1) ^ 1) - 1
            swap_pairs.append((y * grid + i, (other % layers) * grid + i))
    small = pltpu.CompilerParams(vmem_limit_bytes=8 * 2**20)
    limits = pltpu.CompilerParams(vmem_limit_bytes=24 * 2**20)

    in_hbm = pltpu.with_memory_space_constraint(density, pltpu.HBM)
    by_slot = pltpu.with_memory_space_constraint(pattern.T, pltpu.HBM)
    picked = pl.pallas_call(
        pick_kernel,
        out_shape=shape(BS, SHARE * BS),
        in_specs=[HBM],
        out_specs=VMEM,
        scratch_shapes=[pltpu.SemaphoreType.DMA((2,))],
        compiler_params=small,
        name="pick",
    )(in_hbm)
    inner_sent, picked = lax.optimization_barrier((density, picked))
    inner = lax.ppermute(inner_sent, "grid", inner_pairs)
    packing = dict(
        scratch_shapes=[
            pltpu.VMEM(by_slot.shape, jnp.int32),
            pltpu.VMEM((FAR, BS, SPAN), jnp.bfloat16),
            pltpu.VMEM((LISTED, BS), jnp.int32),
            pltpu.SMEM((LISTED, BS), jnp.int32),
            pltpu.VMEM((FAR_BLOCKS + 1, BS, BS), jnp.bfloat16),
            pltpu.SemaphoreType.DMA((3,)),
        ],
        compiler_params=small,
    )
    first_shape, rest_shape = shape(FIRST, BS, BS), shape(REST, BS, BS)
    moves_shape = jax.ShapeDtypeStruct((LISTED, BS), jnp.int32)
    first, moves, unused = pl.pallas_call(
        early_pack_kernel,
        out_shape=(first_shape, moves_shape, rest_shape),
        in_specs=[HBM, HBM],
        out_specs=(ANY, ANY, ANY),
        name="early_pack",
        **packing,
    )(by_slot, in_hbm)
    picked, first = lax.optimization_barrier((picked, first))
    near = lax.ppermute(picked, "grid", outer_pairs)
    first, moves = pl.pallas_call(
        late_pack_kernel,
        out_shape=(first_shape, moves_shape),
        in_specs=[HBM, HBM, ANY, ANY],
        out_specs=(ANY, ANY),
        input_output_aliases={2: 0, 3: 1},
        name="late_pack",
        **packing,
    )(by_slot, in_hbm, first, moves)
    first = lax.ppermute(first, "grid", outer_pairs)

    def send_rest(_):
        rest = pl.pallas_call(
            pack_rest_kernel,
            out_shape=(rest_shape, moves_shape),
            in_specs=[HBM, HBM],
            out_specs=(ANY, ANY),
            name="pack_rest",
            **packing,
        )(by_slot, in_hbm)[0]
        return lax.ppermute(rest, "grid", outer_pairs)

    last = lax.cond(moves[0, BS - 1] > 0, send_rest, lambda blocks: blocks, unused)

    listed, place = tables(pattern, moves)
    near, listed, place, last = lax.optimization_barrier((near, listed, place, last))
    store_shape = shape(STORE, BS, BS)
    out_shape = shape(ROWS, BS, 2 * BS, dtype=jnp.float32)

    def working(rows):
        return [
            pltpu.VMEM((rows, BS, SPAN), jnp.float32),
            pltpu.VMEM((rows, BS, SPAN), jnp.bfloat16),
            pltpu.VMEM((rows, BS, 2 * BS), jnp.float32),
            pltpu.SMEM((ROWS * LISTED,), jnp.int32),
            pltpu.SemaphoreType.DMA((rows,)),
        ]

    swapped = lax.ppermute(near, ("layer", "grid"), swap_pairs)
    store, sums = pl.pallas_call(
        close_kernel,
        out_shape=(store_shape, shape(ROWS, BS, SPAN, dtype=jnp.float32)),
        in_specs=[SMEM, SMEM, HBM, ANY, VMEM, ANY],
        out_specs=(VMEM, VMEM),
        scratch_shapes=[
            pltpu.VMEM(density.shape, density.dtype),
            pltpu.VMEM(density.shape, density.dtype),
            pltpu.SemaphoreType.DMA((3, 4)),
        ],
        compiler_params=limits,
        cost_estimate=cost(4_000_000_000),
        name="close",
    )(listed, place, in_hbm, inner, near, last)
    store, rest, out = pl.pallas_call(
        swapped_kernel,
        out_shape=(store_shape, shape(FAR, BS, SPAN, dtype=jnp.float32), out_shape),
        in_specs=[SMEM, SMEM] + [VMEM] * 4,
        out_specs=(VMEM, VMEM, ANY),
        scratch_shapes=working(NEAR),
        input_output_aliases={5: 0},
        compiler_params=limits,
        cost_estimate=cost(2_000_000_000),
        name="swapped",
    )(listed, place, density, swapped, sums, store)
    return pl.pallas_call(
        far_kernel,
        out_shape=(store_shape, out_shape),
        in_specs=[SMEM, SMEM] + [VMEM] * 4 + [ANY],
        out_specs=(VMEM, ANY),
        scratch_shapes=working(FAR) + [pltpu.SemaphoreType.DMA((1,))],
        input_output_aliases={5: 0, 6: 1},
        compiler_params=limits,
        cost_estimate=cost(2_000_000_000),
        name="far",
    )(listed, place, density, first, rest, store, out)[1]


def solution(mesh):
    placed = (P("grid", None, None), P())
    return jax.shard_map(
        local, mesh=mesh, in_specs=placed, out_specs=P("grid", None, "layer"), check_vma=False
    )
```
